32 devices in a mesh: grp: 2 (over y), lat: 16 (over z, x, core).
Axes of the slice: x: 2, y: 2, z: 4, core: 2. Of those that a mesh axis runs over, the one named last changes fastest.
Arguments:
- state: bfloat16 [128, 72, 128], P(('grp', 'lat')), parts along dimension 0, may hold values from -6 to 6
- tangent: bfloat16 [128, 72, 128], P(('grp', 'lat')), parts along dimension 0, may hold values from -6 to 6
- cotangent: bfloat16 [128, 72, 128], P(('grp', 'lat')), parts along dimension 0, may hold values from -6 to 6
- cubic: bfloat16 [4, 128, 128], replicated, may hold values from -0.25 to 0.25
- w_in: bfloat16 [512, 72], replicated, may hold values from -0.75 to 0.75
- w_out: bfloat16 [72, 512], replicated, may hold values from -0.25 to 0.25
- slots: int32 [4, 64, 4], P('grp', 'lat'), parts along dimension 0, may hold values from 0 to 15, as said below
- sends: int32 [4, 16, 16, 1], P('grp', 'lat'), parts along dimension 0, may hold values from -1 to 3, as said below
Outputs:
- tangent_final: bfloat16 [128, 72, 128], P(('grp', 'lat')), parts along dimension 0
- adjoint_start: float32 [128, 72, 128], P(('grp', 'lat')), parts along dimension 0
- grad_in: float32 [1024, 72], P('grp'), parts along dimension 0
- grad_out: float32 [144, 512], P('grp'), parts along dimension 0
The draws below stay inside these ranges and needn't reach their ends.
There are 2 independent parts, one for each index of `grp`. The reference program is written for one: setup_inputs(seed, part) draws one part's arguments, and reference() takes and returns one part's arrays. A program takes and returns all parts, laid end to end along the dimension named above; an argument that names none is the same for every part. Nothing has to cross between parts.
Inputs may be any that keep to these rules, and one draw needn't show every extreme that they name: On each device d, the 16 entries of one step name distinct slots, 1 from each sender (d + o) mod 16 for every whole o with -8 <= o < 8, and no other slot. `sends`: entry [s, p, d, lane] is the block of sender p that fills slot p + lane of device d at step s; -1 exactly where device d reads nothing from p.
All inputs are finite; a program needn't handle non-finite values.
Results may differ from the reference program's by a relative error of at most 0.013.
Values may be sent and summed in bfloat16 or wider, within the bound.
No kernel may reach another device: no remote copies, remote signals or barrier semaphores. Data moves between devices by JAX's collectives and lax.ppermute only.
A program may use at most 64 MiB of HBM per device.

```python
import jax
import jax.numpy as jnp
from jax import lax

CH = 72
COLS = 128
STENCIL = 4
HID = 512
STEPS = 2
BLK_DEV = 4
PEERS = 16
CAP = 1
BLOCKS = 64
N_LAT = 16


def route_tables(base_key):
    row_count = STENCIL * BLK_DEV
    half_peers = PEERS // 2

    def one_section(section_key):

        def one_device(device_key, device):
            second, third = jax.random.split(device_key, 2)
            owners = ((device + jnp.arange(PEERS, dtype=jnp.int32) - half_peers) % N_LAT).astype(jnp.int32)
            order = jax.random.permutation(second, row_count).astype(jnp.int32)
            chosen = jax.random.randint(third, (PEERS, CAP), 0, BLK_DEV).astype(jnp.int32)
            slot_row = owners[order // CAP] * CAP + order % CAP
            return (slot_row, owners, chosen)
        device_keys = jax.random.split(section_key, N_LAT)
        slot_rows, owners, chosen = jax.vmap(one_device)(device_keys, jnp.arange(N_LAT, dtype=jnp.int32))
        match = owners[:, :, None] == jnp.arange(N_LAT, dtype=jnp.int32)[None, None, :]
        table = jnp.sum(jnp.where(match[:, :, :, None], chosen[:, :, None, :] + 1, 0), axis=1) - 1
        table = jnp.transpose(table, (1, 0, 2)).astype(jnp.int32)
        return (slot_rows.reshape(N_LAT * BLK_DEV, STENCIL), table)
    section_keys = jax.random.split(base_key, STEPS)
    return jax.vmap(one_section)(section_keys)


def draw_slots(key, part):
    tables = route_tables(key)
    return tables[0]


def draw_sends(key, part):
    tables = route_tables(key)
    return tables[1]


def shard_levels(stream_key, extent, shards, smallest, top_value):
    def one(dim, shards_of):
        draws = jax.random.uniform(jax.random.fold_in(jax.random.fold_in(stream_key, 6), dim), (shards_of,), jnp.float32, smallest / len(shards), top_value / len(shards))
        return jnp.repeat(jnp.exp(draws), extent[dim] // shards_of).reshape((-1,) + (1,) * (len(extent) - dim - 1))

    gain = one(*shards[0])
    for cut in shards[1:]:
        gain = gain * one(*cut)
    return gain


def normal_values(key, extent, spread, bound, shards=(), kind=jnp.bfloat16):
    values = jax.random.normal(key, extent, jnp.float32) * spread
    if len(shards) > 0:
        values = shard_levels(key, extent, shards, -0.22, 0.18) * values
    return jnp.clip(values, min=-bound, max=bound).astype(kind)


def setup_inputs(seed: int = 0, part: int = 0) -> dict:
    splits = jax.random.split(jax.random.key(seed), 9)
    part_keys = jax.random.split(jax.random.fold_in(splits[8], part), 9)
    state = normal_values(part_keys[0], (BLOCKS, CH, COLS), 1.0, 6.0, ((0, 16),))
    tangent = normal_values(part_keys[1], (BLOCKS, CH, COLS), 1.0, 6.0, ((0, 16),))
    cotangent = normal_values(part_keys[2], (BLOCKS, CH, COLS), 1.0, 6.0, ((0, 16),))
    cubic = normal_values(splits[3], (STENCIL, COLS, COLS), (STENCIL * COLS) ** -0.5, 0.25)
    w_in = normal_values(splits[4], (HID, CH), CH ** -0.5, 0.75)
    w_out = normal_values(splits[5], (CH, HID), HID ** -0.5, 0.25)
    slots = draw_slots(jax.random.fold_in(jax.random.fold_in(splits[8], part), 71), part)
    sends = draw_sends(jax.random.fold_in(jax.random.fold_in(splits[8], part), 71), part)
    return {"state": state, "tangent": tangent, "cotangent": cotangent, "cubic": cubic, "w_in": w_in, "w_out": w_out, "slots": slots, "sends": sends}


def silu_slope(preact):
    sigma = jax.nn.sigmoid(preact)
    return sigma * (1.0 + preact * (1.0 - sigma))


def route_sources(slot_table, send_table):
    device = (jnp.arange(BLOCKS, dtype=jnp.int32) // BLK_DEV)[:, None]
    sender = slot_table // CAP
    lane_idx = slot_table % CAP
    entry = send_table[sender, device, lane_idx]
    valid = entry >= 0
    source = (sender * BLK_DEV + jnp.maximum(entry, 0)).astype(jnp.int32)
    return source, valid


def advect_group(field, source, valid, cubic):
    picked = field[source]
    picked = jnp.where(valid[:, :, None, None], picked, jnp.zeros((), field.dtype))
    return jnp.einsum('bkcn,knm->bcm', picked.astype(jnp.float32), cubic.astype(jnp.float32)).astype(jnp.bfloat16)


def forward_step(field, pert, source, valid, cubic, w_in, w_out):
    win32 = w_in.astype(jnp.float32)
    wout32 = w_out.astype(jnp.float32)

    def one_group(group):
        src, val = group
        advected = advect_group(field, src, val, cubic)
        tadv = advect_group(pert, src, val, cubic)
        preact = jnp.einsum('hc,bcn->bhn', win32, advected.astype(jnp.float32))
        hidden = jax.nn.silu(preact).astype(jnp.bfloat16)
        newx = (advected.astype(jnp.float32) + jnp.einsum('ch,bhn->bcn', wout32, hidden.astype(jnp.float32))).astype(jnp.bfloat16)
        thid = (silu_slope(preact) * jnp.einsum('hc,bcn->bhn', win32, tadv.astype(jnp.float32))).astype(jnp.bfloat16)
        newt = (tadv.astype(jnp.float32) + jnp.einsum('ch,bhn->bcn', wout32, thid.astype(jnp.float32))).astype(jnp.bfloat16)
        return advected, newx, newt

    advected, newx, newt = lax.map(one_group, (source.reshape(N_LAT, BLK_DEV, STENCIL), valid.reshape(N_LAT, BLK_DEV, STENCIL)))
    shape = (BLOCKS, CH, COLS)
    return advected.reshape(shape), newx.reshape(shape), newt.reshape(shape)


def backward_step(advected, lam, source, valid, cubic, w_in, w_out):
    win32 = w_in.astype(jnp.float32)
    wout32 = w_out.astype(jnp.float32)
    cub32 = cubic.astype(jnp.float32)

    def one_group(total, group):
        adv, lamg, src, val = group
        adv32 = adv.astype(jnp.float32)
        lam32 = lamg.astype(jnp.float32)
        preact = jnp.einsum('hc,bcn->bhn', win32, adv32)
        hidden = jax.nn.silu(preact).astype(jnp.bfloat16)
        ghid = (silu_slope(preact) * jnp.einsum('ch,bcn->bhn', wout32, lam32)).astype(jnp.bfloat16)
        ladv = (lam32 + jnp.einsum('hc,bhn->bcn', win32, ghid.astype(jnp.float32))).astype(jnp.bfloat16)
        gin = jnp.einsum('bhn,bcn->hc', ghid.astype(jnp.float32), adv32)
        gout = jnp.einsum('bcn,bhn->ch', lam32, hidden.astype(jnp.float32))
        terms = jnp.einsum('bcm,knm->bkcn', ladv.astype(jnp.float32), cub32).astype(jnp.bfloat16).astype(jnp.float32)
        terms = jnp.where(val[:, :, None, None], terms, jnp.zeros((), jnp.float32))
        back, gin_sum, gout_sum = total
        back = back.at[src.reshape(-1)].add(terms.reshape(-1, CH, COLS))
        return (back, gin_sum + gin, gout_sum + gout), None

    shape = (N_LAT, BLK_DEV, CH, COLS)
    init = (jnp.zeros((BLOCKS, CH, COLS), jnp.float32), jnp.zeros((HID, CH), jnp.float32), jnp.zeros((CH, HID), jnp.float32))
    groups = (advected.reshape(shape), lam.reshape(shape), source.reshape(N_LAT, BLK_DEV, STENCIL), valid.reshape(N_LAT, BLK_DEV, STENCIL))
    result, unused = lax.scan(one_group, init, groups)
    return result


def reference(state, tangent, cotangent, cubic, w_in, w_out, slots, sends):
    field, pert = state, tangent
    saved = []
    routes = []
    for section in range(STEPS):
        source, valid = route_sources(slots[section], sends[section])
        routes.append((source, valid))
        advected, field, pert = forward_step(field, pert, source, valid, cubic, w_in, w_out)
        saved.append(advected)
    lam = cotangent
    grad_in = jnp.zeros((HID, CH), jnp.float32)
    grad_out = jnp.zeros((CH, HID), jnp.float32)
    back = None
    for section in reversed(range(STEPS)):
        source, valid = routes[section]
        back, gin, gout = backward_step(saved[section], lam, source, valid, cubic, w_in, w_out)
        grad_in = grad_in + gin
        grad_out = grad_out + gout
        lam = back.astype(jnp.bfloat16)
    return pert, back, grad_in, grad_out
```

```python
import functools

import jax
import jax.numpy as jnp
from jax import lax
from jax.experimental import pallas as pl
from jax.experimental.pallas import tpu as pltpu
from jax.sharding import PartitionSpec as P

BF = jnp.bfloat16
F32 = jnp.float32


def call(kernel, outs, tables, arrays, flops):
    moved = sum(a.size * a.dtype.itemsize for a in arrays)
    moved += sum(o.size * o.dtype.itemsize for o in outs)
    return pl.pallas_call(
        kernel,
        out_shape=tuple(outs),
        in_specs=[pl.BlockSpec(memory_space=pltpu.SMEM)] * len(tables)
        + [pl.BlockSpec(memory_space=pltpu.VMEM)] * len(arrays),
        out_specs=tuple(pl.BlockSpec(memory_space=pltpu.VMEM) for _ in outs),
        compiler_params=pltpu.CompilerParams(vmem_limit_bytes=32 * 1024 * 1024),
        cost_estimate=pl.CostEstimate(flops=flops, bytes_accessed=moved, transcendentals=0),
    )(*tables, *arrays)


def shape(dims, dtype=BF):
    return jax.ShapeDtypeStruct(tuple(dims), dtype)


def dot(a, b):
    return jnp.dot(a, b, preferred_element_type=F32)


def dot_nt(a, b):
    return lax.dot_general(a, b, (((1,), (1,)), ((), ())), preferred_element_type=F32)


def to_rows(wide, count):
    width = wide.shape[1] // count
    return jnp.concatenate([wide[:, j * width : (j + 1) * width] for j in range(count)], axis=0)


def to_lanes(tall, count):
    height = tall.shape[0] // count
    return jnp.concatenate([tall[j * height : (j + 1) * height] for j in range(count)], axis=1)


def gates(preact):
    sigma = 0.5 + 0.5 * jnp.tanh(0.5 * preact)
    hidden = preact * sigma
    return hidden, sigma + hidden * (1.0 - sigma)


def advect(read, slots_ref, section, count, stencil, cubic_ref):
    parts = []
    for k in range(stencil):
        rows = [read(slots_ref[(section * count + j) * stencil + k]).astype(F32) for j in range(count)]
        parts.append(jnp.concatenate(rows, axis=0).astype(BF))
    return to_lanes(dot(jnp.concatenate(parts, axis=1), cubic_ref[...]), count)


def scatter_terms(ladv, count, stencil, section, slots_ref, cubic_t_ref, write):
    width = ladv.shape[1] // count
    height = ladv.shape[0]
    terms = dot(to_rows(ladv, count).astype(BF), cubic_t_ref[...])
    for j in range(count):
        for k in range(stencil):
            block = terms[j * height : (j + 1) * height, k * width : (k + 1) * width]
            write(slots_ref[(section * count + j) * stencil + k], block.astype(BF))


def pack(sends_ref, section, slots, read, write):
    def one(q):
        write(q, read(jnp.maximum(sends_ref[section * slots + q], 0)))

    if slots <= 16:
        for q in range(slots):
            one(q)
    else:
        pl.loop(0, slots)(one)


def collect(sends_ref, section, slots, read, total_ref):
    total_ref[...] = jnp.zeros(total_ref.shape, F32)

    def one(q):
        entry = sends_ref[section * slots + q]

        @pl.when(entry >= 0)
        def _():
            total_ref[entry] += read(q).astype(F32)

    if slots <= 16:
        for q in range(slots):
            one(q)
    else:
        pl.loop(0, slots)(one)


def pack_kernel(slots, sends_ref, state_ref, tangent_ref, out_ref):
    def write_state(q, block):
        out_ref[q, 0] = block

    def write_tangent(q, block):
        out_ref[q, 1] = block

    pack(sends_ref, 0, slots, lambda e: state_ref[e], write_state)
    pack(sends_ref, 0, slots, lambda e: tangent_ref[e], write_tangent)


def prepare_kernel(w_in_ref, w_out_ref, cubic_ref, cot_ref, w_in_t_ref, w_out_t_ref, cubic_t_ref, lam_ref, pull_ref):
    count = cot_ref.shape[0]
    columns = cubic_ref.shape[1]
    w_in_t_ref[...] = w_in_ref[...].astype(F32).T.astype(BF)
    w_out_t = w_out_ref[...].astype(F32).T.astype(BF)
    w_out_t_ref[...] = w_out_t
    for k in range(cubic_ref.shape[0] // columns):
        tile = cubic_ref[k * columns : (k + 1) * columns, :].astype(F32)
        cubic_t_ref[:, k * columns : (k + 1) * columns] = tile.T.astype(BF)
    lam = jnp.concatenate([cot_ref[j] for j in range(count)], axis=1)
    lam_ref[...] = lam
    pull_ref[...] = dot(w_out_t, lam)


def first_kernel(count, stencil, slots, slots_ref, sends_ref, recv_ref, cubic_ref, w_in_ref, w_out_ref,
                 send_ref, adv_ref, hidden_ref, slope_ref, field_ref):
    adv = advect(lambda q: recv_ref[q, 0], slots_ref, 0, count, stencil, cubic_ref).astype(BF)
    adv_ref[...] = adv
    hidden, slope = gates(dot(w_in_ref[...], adv))
    hidden = hidden.astype(BF)
    field = adv.astype(F32) + dot(w_out_ref[...], hidden)
    width = field.shape[1] // count
    for j in range(count):
        field_ref[j] = field[:, j * width : (j + 1) * width].astype(BF)

    def write(q, block):
        send_ref[q] = block

    pack(sends_ref, 1, slots, lambda e: field_ref[e], write)
    hidden_ref[...] = hidden
    slope_ref[...] = slope


def tangent_kernel(section, count, stencil, slots_ref, recv_ref, cubic_ref, w_in_ref, w_out_ref, slope_ref, out_ref):
    tadv = advect(lambda q: recv_ref[q, 1], slots_ref, section, count, stencil, cubic_ref).astype(BF)
    thid = (slope_ref[...] * dot(w_in_ref[...], tadv)).astype(BF)
    pert = tadv.astype(F32) + dot(w_out_ref[...], thid)
    width = pert.shape[1] // count
    for j in range(count):
        out_ref[j] = pert[:, j * width : (j + 1) * width].astype(BF)


def second_kernel(count, stencil, slots, slots_ref, recv_ref, cubic_ref, cubic_t_ref, w_in_ref, w_in_t_ref, lam_ref, pull_ref,
                  send_ref, adv_ref, hidden_ref, slope_ref, ghid_ref):
    adv = advect(lambda q: recv_ref[q], slots_ref, 1, count, stencil, cubic_ref).astype(BF)
    adv_ref[...] = adv
    hidden, slope = gates(dot(w_in_ref[...], adv))
    hidden_ref[...] = hidden.astype(BF)
    slope_ref[...] = slope
    ghid = (slope * pull_ref[...]).astype(BF)
    ghid_ref[...] = ghid
    ladv = lam_ref[...].astype(F32) + dot(w_in_t_ref[...], ghid)
    if slots != count * stencil:
        send_ref[...] = jnp.zeros(send_ref.shape, BF)

    def write(q, block):
        send_ref[q] = block

    scatter_terms(ladv, count, stencil, 1, slots_ref, cubic_t_ref, write)


def grad_kernel(lam_ref, hidden_ref, ghid_ref, adv_ref, in_ref, out_ref):
    in_ref[...] = dot_nt(adv_ref[...], ghid_ref[...])
    out_ref[...] = dot_nt(lam_ref[...], hidden_ref[...])


def third_kernel(count, stencil, slots, slots_ref, sends_ref, recv_ref, cubic_t_ref, w_in_t_ref, w_out_t_ref, slope_ref, pert_ref,
                 send_ref, lam_ref, ghid_ref, total_ref):
    collect(sends_ref, 1, slots, lambda q: recv_ref[q], total_ref)
    lam = jnp.concatenate([total_ref[j] for j in range(count)], axis=1).astype(BF)
    lam_ref[...] = lam
    ghid = (slope_ref[...] * dot(w_out_t_ref[...], lam)).astype(BF)
    ghid_ref[...] = ghid
    ladv = lam.astype(F32) + dot(w_in_t_ref[...], ghid)
    if slots != count * stencil:
        send_ref[...] = jnp.zeros(send_ref.shape, BF)

    def write_term(q, block):
        send_ref[q, 0] = block

    def write_pert(q, block):
        send_ref[q, 1] = block

    scatter_terms(ladv, count, stencil, 0, slots_ref, cubic_t_ref, write_term)
    pack(sends_ref, 1, slots, lambda e: pert_ref[e], write_pert)


def grad_pair_kernel(side_ref, lam_ref, hidden_ref, ghid_ref, adv_ref, in_ref, out_ref, keep_ref, give_ref):
    grad_in = (in_ref[...] + dot_nt(adv_ref[...], ghid_ref[...])).astype(BF)
    grad_out = (out_ref[...] + dot_nt(lam_ref[...], hidden_ref[...])).astype(BF)

    @pl.when(side_ref[0] == 0)
    def _():
        keep_ref[...] = grad_in
        give_ref[...] = grad_out

    @pl.when(side_ref[0] != 0)
    def _():
        keep_ref[...] = grad_out
        give_ref[...] = grad_in


def last_kernel(count, stencil, slots, slots_ref, sends_ref, recv_ref, cubic_ref, w_in_ref, w_out_ref, slope_ref, back_ref, pert_ref):
    collect(sends_ref, 0, slots, lambda q: recv_ref[q, 0], back_ref)
    tangent_kernel(1, count, stencil, slots_ref, recv_ref, cubic_ref, w_in_ref, w_out_ref, slope_ref, pert_ref)


def grad_end_kernel(side_ref, mine_ref, other_ref, in_ref, out_ref):
    mine = mine_ref[...].astype(F32)
    other = other_ref[...].astype(F32)

    @pl.when(side_ref[0] == 0)
    def _():
        in_ref[...] = mine.T
        out_ref[...] = other

    @pl.when(side_ref[0] != 0)
    def _():
        in_ref[...] = other.T
        out_ref[...] = mine


def shards(state, tangent, cotangent, cubic, w_in, w_out, slots, sends):
    count, channels, columns = state.shape
    stencil = cubic.shape[0]
    hid = w_in.shape[0]
    peers = lax.axis_size("lat")
    slot_count = peers * sends.shape[-1]
    wide = count * columns
    blocks = (count, channels, columns)
    me = lax.axis_index("lat")
    side = (me % 2).astype(jnp.int32).reshape(1)
    slots = slots.reshape(-1)
    sends = sends.reshape(-1)
    cubic = cubic.reshape(stencil * columns, columns)
    mix = 2 * wide * channels * stencil * columns
    net = 2 * wide * channels * hid
    sizes = (count, stencil, slot_count)

    def exchange(packed):
        return lax.all_to_all(packed, "lat", split_axis=0, concat_axis=0, tiled=True)

    def swap(values, step):
        return lax.ppermute(values, "lat", [(i, i ^ step) for i in range(peers)])

    (send,) = call(
        functools.partial(pack_kernel, slot_count),
        [shape((slot_count, 2, channels, columns))], [sends], [state, tangent], 0,
    )
    recv_one = exchange(send)
    w_in_t, w_out_t, cubic_t, lam_two, pull_two = call(
        prepare_kernel,
        [shape((channels, hid)), shape((hid, channels)), shape((columns, stencil * columns)),
         shape((channels, wide)), shape((hid, wide), F32)],
        [], [w_in, w_out, cubic, cotangent], net,
    )
    send, adv_one, hidden_one, slope_one, _ = call(
        functools.partial(first_kernel, *sizes),
        [shape((slot_count, channels, columns)), shape((channels, wide)), shape((hid, wide)), shape((hid, wide), F32), shape(blocks)],
        [slots, sends], [recv_one, cubic, w_in, w_out], mix + 2 * net,
    )
    recv_two = exchange(send)
    (pert_one,) = call(
        functools.partial(tangent_kernel, 0, count, stencil),
        [shape(blocks)], [slots], [recv_one, cubic, w_in, w_out, slope_one], mix + 2 * net,
    )
    send, adv_two, hidden_two, slope_two, ghid_two = call(
        functools.partial(second_kernel, *sizes),
        [shape((slot_count, channels, columns)), shape((channels, wide)), shape((hid, wide)), shape((hid, wide), F32), shape((hid, wide))],
        [slots], [recv_two, cubic, cubic_t, w_in, w_in_t, lam_two, pull_two], 2 * mix + 2 * net,
    )
    recv_three = exchange(send)
    part_in, part_out = call(
        grad_kernel,
        [shape((channels, hid), F32)] * 2, [], [lam_two, hidden_two, ghid_two, adv_two], 2 * net,
    )
    send, lam_one, ghid_one, _ = call(
        functools.partial(third_kernel, *sizes),
        [shape((slot_count, 2, channels, columns)), shape((channels, wide)), shape((hid, wide)), shape(blocks, F32)],
        [slots, sends], [recv_three, cubic_t, w_in_t, w_out_t, slope_one, pert_one], mix + 2 * net,
    )
    recv_four = exchange(send)
    mine, give = call(
        grad_pair_kernel,
        [shape((channels, hid))] * 2, [side], [lam_one, hidden_one, ghid_one, adv_one, part_in, part_out], 2 * net,
    )
    mine = (mine.astype(F32) + swap(give, 1).astype(F32)).astype(BF)
    step = 2
    while step < peers:
        mine = (mine.astype(F32) + swap(mine, step).astype(F32)).astype(BF)
        step *= 2
    grad_in, grad_out = call(
        grad_end_kernel,
        [shape((hid, channels), F32), shape((channels, hid), F32)], [side], [mine, swap(mine, 1)], 0,
    )
    back, pert = call(
        functools.partial(last_kernel, *sizes),
        [shape(blocks, F32), shape(blocks)],
        [slots, sends], [recv_four, cubic, w_in, w_out, slope_two], mix + 2 * net,
    )
    return (pert, back, grad_in, grad_out)


def solution(mesh):
    in_specs = (
        P(("grp", "lat"), None, None),
        P(("grp", "lat"), None, None),
        P(("grp", "lat"), None, None),
        P(),
        P(),
        P(),
        P("grp", "lat", None),
        P("grp", "lat", None, None),
    )
    out_specs = (
        P(("grp", "lat"), None, None),
        P(("grp", "lat"), None, None),
        P("grp", None),
        P("grp", None),
    )
    return jax.shard_map(shards, mesh=mesh, in_specs=in_specs, out_specs=out_specs, check_vma=False)
```

```python
import functools

import jax
import jax.numpy as jnp
from jax import lax
from jax.experimental import pallas as pl
from jax.experimental.pallas import tpu as pltpu
from jax.sharding import PartitionSpec as P

BF = jnp.bfloat16
F32 = jnp.float32
VMEM = pltpu.VMEM
HBM = pltpu.HBM


def shape(dims, dtype=BF):
    return jax.ShapeDtypeStruct(tuple(dims), dtype)


class Placed:
    def __init__(self, memory_space, dims, dtype=BF):
        self.memory_space, self.shape, self.dtype = memory_space, tuple(dims), jnp.dtype(dtype)
        self.size = functools.reduce(lambda a, b: a * b, self.shape, 1)


SMEM = pltpu.SMEM


def call(kernel, outs, tables, arrays, flops, scratch=()):
    moved = sum(a.size * a.dtype.itemsize for a in arrays) + sum(o.size * o.dtype.itemsize for o in outs)
    places = [o.memory_space if isinstance(o, Placed) else VMEM for o in outs]
    return pl.pallas_call(
        kernel,
        out_shape=tuple(o.memory_space(o.shape, o.dtype) if isinstance(o, Placed) else o for o in outs),
        in_specs=[pl.BlockSpec(memory_space=SMEM)] * len(tables) + [pl.BlockSpec(memory_space=VMEM)] * len(arrays),
        out_specs=tuple(pl.BlockSpec(memory_space=place) for place in places),
        scratch_shapes=list(scratch),
        compiler_params=pltpu.CompilerParams(vmem_limit_bytes=32 * 1024 * 1024),
        cost_estimate=pl.CostEstimate(flops=flops, bytes_accessed=moved, transcendentals=0),
    )(*tables, *arrays)


def dot(a, b):
    return jnp.dot(a, b, preferred_element_type=F32)


def dot_nt(a, b):
    return lax.dot_general(a, b, (((1,), (1,)), ((), ())), preferred_element_type=F32)


def to_rows(wide, count):
    width = wide.shape[1] // count
    return jnp.concatenate([wide[:, j * width : (j + 1) * width] for j in range(count)], axis=0)


def to_lanes(tall, count):
    height = tall.shape[0] // count
    return jnp.concatenate([tall[j * height : (j + 1) * height] for j in range(count)], axis=1)


def gates(preact):
    sigma = 0.5 + 0.5 * jnp.tanh(0.5 * preact)
    hidden = preact * sigma
    return hidden, sigma + hidden * (1.0 - sigma)


def repeat(slots, one):
    if slots <= 16:
        for q in range(slots):
            one(q)
    else:
        pl.loop(0, slots)(one)


def advect(read, slots_ref, section, count, stencil, cubic_ref):
    parts = []
    for k in range(stencil):
        rows = [read(slots_ref[section, j, k]).astype(F32) for j in range(count)]
        parts.append(jnp.concatenate(rows, axis=0).astype(BF))
    return to_lanes(dot(jnp.concatenate(parts, axis=1), cubic_ref[...]), count)


def entry_of(sends_ref, section, q):
    cap = sends_ref.shape[2]
    return sends_ref[section, 0, q % cap, q // cap]


def send_blocks(sends_ref, section, slots, source_ref, target, sem):
    def one(q):
        entry = jnp.maximum(entry_of(sends_ref, section, q), 0)
        pltpu.make_async_copy(source_ref.at[entry], target(q), sem).start()

    repeat(slots, one)


def send_terms(ladv, count, stencil, section, slots_ref, cubic_ref, terms_ref, target, sem):
    width = ladv.shape[1] // count
    height = ladv.shape[0]
    terms = dot_nt(to_rows(ladv, count).astype(BF), cubic_ref[...])
    for j in range(count):
        for k in range(stencil):
            block = terms[j * height : (j + 1) * height, k * width : (k + 1) * width]
            terms_ref[j * stencil + k] = block.astype(BF)
            pltpu.make_async_copy(terms_ref.at[j * stencil + k], target(slots_ref[section, j, k]), sem).start()


def collect(sends_ref, section, slots, read, total_ref):
    total_ref[...] = jnp.zeros(total_ref.shape, F32)

    def one(q):
        entry = entry_of(sends_ref, section, q)

        @pl.when(entry >= 0)
        def _():
            total_ref[entry] += read(q).astype(F32)

    repeat(slots, one)


def pack_kernel(slots, slots_in_ref, sends_in_ref, state_in_ref, tangent_in_ref, out_ref, slots_ref, sends_ref,
                state_ref, tangent_ref, in_sems, sem):
    pairs = ((sends_in_ref, sends_ref), (state_in_ref, state_ref), (tangent_in_ref, tangent_ref), (slots_in_ref, slots_ref))
    loads = [pltpu.make_async_copy(a, b, in_sems.at[i]) for i, (a, b) in enumerate(pairs)]
    for load in loads:
        load.start()
    loads[0].wait()
    loads[1].wait()
    send_blocks(sends_ref, 0, slots, state_ref, lambda q: out_ref.at[q, 0], sem)
    loads[2].wait()
    send_blocks(sends_ref, 0, slots, tangent_ref, lambda q: out_ref.at[q, 1], sem)
    loads[3].wait()
    pltpu.make_async_copy(out_ref, out_ref, sem).wait()


def prepare_kernel(w_in_t_ref, w_out_ref, w_in_ref, w_out_t_ref):
    w_in_ref[...] = w_in_t_ref[...].astype(F32).T.astype(BF)
    w_out_t_ref[...] = w_out_ref[...].astype(F32).T.astype(BF)


def first_kernel(count, stencil, slots, slots_ref, sends_ref, recv_ref, cubic_ref, w_in_ref, w_out_ref,
                 send_ref, adv_ref, field_ref, sem):
    adv = advect(lambda q: recv_ref[q, 0], slots_ref, 0, count, stencil, cubic_ref).astype(BF)
    adv_ref[...] = adv
    hidden = gates(dot(w_in_ref[...], adv))[0].astype(BF)
    field = adv.astype(F32) + dot(w_out_ref[...], hidden)
    width = field.shape[1] // count
    for j in range(count):
        field_ref[j] = field[:, j * width : (j + 1) * width].astype(BF)
    send_blocks(sends_ref, 1, slots, field_ref, lambda q: send_ref.at[q], sem)
    pltpu.make_async_copy(send_ref, send_ref, sem).wait()


def tangent_kernel(section, count, stencil, slots_ref, recv_ref, cubic_ref, w_in_ref, w_out_ref, adv_ref, out_ref):
    slope = gates(dot(w_in_ref[...], adv_ref[...]))[1]
    tadv = advect(lambda q: recv_ref[q, 1], slots_ref, section, count, stencil, cubic_ref).astype(BF)
    thid = (slope * dot(w_in_ref[...], tadv)).astype(BF)
    pert = tadv.astype(F32) + dot(w_out_ref[...], thid)
    width = pert.shape[1] // count
    for j in range(count):
        out_ref[j] = pert[:, j * width : (j + 1) * width].astype(BF)


def side_by_side(ref):
    return jnp.concatenate([ref[j] for j in range(ref.shape[0])], axis=1)


def second_kernel(count, stencil, slots, slots_ref, recv_ref, cubic_ref, w_in_ref, w_in_t_ref, w_out_t_ref, cot_ref,
                  send_ref, adv_ref, terms_ref, sem):
    lam = side_by_side(cot_ref)
    adv = advect(lambda q: recv_ref[q], slots_ref, 1, count, stencil, cubic_ref).astype(BF)
    adv_ref[...] = adv
    slope = gates(dot(w_in_ref[...], adv))[1]
    ghid = (slope * dot(w_out_t_ref[...], lam)).astype(BF)
    ladv = lam.astype(F32) + dot(w_in_t_ref[...], ghid)
    send_terms(ladv, count, stencil, 1, slots_ref, cubic_ref, terms_ref, lambda q: send_ref.at[q], sem)
    pltpu.make_async_copy(terms_ref, terms_ref, sem).wait()


def between_kernel(cot_ref, w_in_ref, w_out_t_ref, adv_two_ref, adv_one_ref, in_ref, out_ref, hidden_ref, slope_ref):
    lam = side_by_side(cot_ref)
    adv = adv_two_ref[...]
    hidden, slope = gates(dot(w_in_ref[...], adv))
    ghid = (slope * dot(w_out_t_ref[...], lam)).astype(BF)
    in_ref[...] = dot_nt(adv, ghid)
    out_ref[...] = dot_nt(lam, hidden.astype(BF))
    hidden, slope = gates(dot(w_in_ref[...], adv_one_ref[...]))
    hidden_ref[...] = hidden.astype(BF)
    slope_ref[...] = slope.astype(BF)


def third_kernel(count, stencil, slots, slots_ref, sends_ref, recv_ref, cubic_ref, w_in_t_ref, w_out_t_ref, slope_ref, pert_ref,
                 send_ref, lam_ref, ghid_ref, total_ref, terms_ref, sems):
    send_blocks(sends_ref, 1, slots, pert_ref, lambda q: send_ref.at[q, 1], sems.at[1])
    collect(sends_ref, 1, slots, lambda q: recv_ref[q], total_ref)
    lam = side_by_side(total_ref).astype(BF)
    lam_ref[...] = lam
    ghid = (slope_ref[...].astype(F32) * dot(w_out_t_ref[...], lam)).astype(BF)
    ghid_ref[...] = ghid
    ladv = lam.astype(F32) + dot(w_in_t_ref[...], ghid)
    send_terms(ladv, count, stencil, 0, slots_ref, cubic_ref, terms_ref, lambda q: send_ref.at[q, 0], sems.at[0])
    pltpu.make_async_copy(terms_ref, terms_ref, sems.at[0]).wait()
    half = send_ref.at[pl.ds(0, slots // 2)]
    pltpu.make_async_copy(half, half, sems.at[1]).wait()


def grad_pair_kernel(side_ref, lam_ref, hidden_ref, ghid_ref, adv_ref, in_ref, out_ref, keep_ref, give_ref):
    grad_in = (in_ref[...] + dot_nt(adv_ref[...], ghid_ref[...])).astype(BF)
    grad_out = (out_ref[...] + dot_nt(lam_ref[...], hidden_ref[...])).astype(BF)

    @pl.when(side_ref[0] == 0)
    def _():
        keep_ref[...] = grad_in
        give_ref[...] = grad_out

    @pl.when(side_ref[0] != 0)
    def _():
        keep_ref[...] = grad_out
        give_ref[...] = grad_in


def last_kernel(count, stencil, slots, slots_ref, sends_ref, recv_ref, cubic_ref, w_in_ref, w_out_ref, adv_ref, back_ref, pert_ref):
    collect(sends_ref, 0, slots, lambda q: recv_ref[q, 0], back_ref)
    tangent_kernel(1, count, stencil, slots_ref, recv_ref, cubic_ref, w_in_ref, w_out_ref, adv_ref, pert_ref)


def shards(state, tangent, cotangent, cubic, w_in, w_out, slots, sends):
    count, channels, columns = state.shape
    stencil = cubic.shape[0]
    hid = w_in.shape[0]
    peers = lax.axis_size("lat")
    slot_count = peers * sends.shape[-1]
    wide = count * columns
    block = (channels, columns)
    blocks = (count, *block)
    side = lax.axis_index("lat") % 2
    sends = jnp.transpose(sends, (0, 1, 3, 2))
    cubic = cubic.reshape(stencil * columns, columns)
    w_in_t = w_in.T
    mix = 2 * wide * channels * stencil * columns
    net = 2 * wide * channels * hid
    sizes = (count, stencil, slot_count)
    sem = pltpu.SemaphoreType.DMA

    def exchange(packed):
        return lax.all_to_all(packed, "lat", split_axis=0, concat_axis=0, tiled=True)

    def swap(values, step):
        return lax.ppermute(values, "lat", [(i, i ^ step) for i in range(peers)])

    def add(a, b):
        return (a.astype(F32) + b.astype(F32)).astype(BF)

    send, slots, sends = pl.pallas_call(
        functools.partial(pack_kernel, slot_count),
        out_shape=(HBM((slot_count, 2, *block), BF), SMEM(slots.shape, slots.dtype), SMEM(sends.shape, sends.dtype)),
        in_specs=[pl.BlockSpec(memory_space=HBM)] * 4,
        out_specs=(pl.BlockSpec(memory_space=HBM), pl.BlockSpec(memory_space=SMEM), pl.BlockSpec(memory_space=SMEM)),
        scratch_shapes=[VMEM(blocks, BF), VMEM(blocks, BF), sem((4,)), sem],
    )(*(pltpu.with_memory_space_constraint(a, HBM) for a in (slots, sends, state, tangent)))
    recv_one = exchange(send)
    w_in, w_out_t = call(prepare_kernel, [shape((hid, channels)), shape((hid, channels))], [], [w_in_t, w_out], 0)
    send, adv_one = call(
        functools.partial(first_kernel, *sizes),
        [Placed(HBM, (slot_count, *block)), shape((channels, wide))],
        [slots, sends], [recv_one, cubic, w_in, w_out], mix + 2 * net, [VMEM(blocks, BF), sem],
    )
    recv_two = exchange(send)
    (pert_one,) = call(
        functools.partial(tangent_kernel, 0, count, stencil),
        [shape(blocks)], [slots], [recv_one, cubic, w_in, w_out, adv_one], mix + 3 * net,
    )
    recv_two, pert_one = lax.optimization_barrier((recv_two, pert_one))
    send, adv_two = call(
        functools.partial(second_kernel, *sizes),
        [Placed(HBM, (slot_count, *block)), shape((channels, wide))],
        [slots], [recv_two, cubic, w_in, w_in_t, w_out_t, cotangent], 2 * mix + 3 * net,
        [VMEM((count * stencil, *block), BF), sem],
    )
    recv_three = exchange(send)
    part_in, part_out, hidden_one, slope_one = call(
        between_kernel,
        [shape((channels, hid), F32)] * 2 + [shape((hid, wide))] * 2,
        [], [cotangent, w_in, w_out_t, adv_two, adv_one], 5 * net,
    )
    send, lam_one, ghid_one = call(
        functools.partial(third_kernel, *sizes),
        [Placed(HBM, (slot_count, 2, *block)), shape((channels, wide)), shape((hid, wide))],
        [slots, sends], [recv_three, cubic, w_in_t, w_out_t, slope_one, pert_one], mix + 2 * net,
        [VMEM(blocks, F32), VMEM((count * stencil, *block), BF), sem((2,))],
    )
    recv_four = exchange(send)
    mine, give = call(
        grad_pair_kernel,
        [shape((channels, hid))] * 2, [side.astype(jnp.int32).reshape(1)],
        [lam_one, hidden_one, ghid_one, adv_one, part_in, part_out], 2 * net,
    )
    mine = add(mine, swap(give, 1))
    step = 2
    while step < peers:
        mine = add(mine, swap(mine, step))
        step *= 2
    mine, recv_four = lax.optimization_barrier((mine, recv_four))
    back, pert = call(
        functools.partial(last_kernel, *sizes),
        [shape(blocks, F32), shape(blocks)],
        [slots, sends], [recv_four, cubic, w_in, w_out, adv_two], mix + 3 * net,
    )
    other = swap(mine, 1)
    grad_in = jnp.where(side == 0, mine, other).astype(F32).T
    grad_out = jnp.where(side == 0, other, mine).astype(F32)
    return (pert, back, grad_in, grad_out)


def solution(mesh):
    in_specs = (
        P(("grp", "lat"), None, None),
        P(("grp", "lat"), None, None),
        P(("grp", "lat"), None, None),
        P(),
        P(),
        P(),
        P("grp", "lat", None),
        P("grp", "lat", None, None),
    )
    out_specs = (
        P(("grp", "lat"), None, None),
        P(("grp", "lat"), None, None),
        P("grp", None),
        P("grp", None),
    )
    return jax.shard_map(shards, mesh=mesh, in_specs=in_specs, out_specs=out_specs, check_vma=False)
```

```python
import functools

import jax
import jax.numpy as jnp
from jax import lax
from jax.experimental import pallas as pl
from jax.experimental.pallas import tpu as pltpu
from jax.sharding import PartitionSpec as P

BF = jnp.bfloat16
F32 = jnp.float32
VMEM = pltpu.VMEM
HBM = pltpu.HBM


def shape(dims, dtype=BF):
    return jax.ShapeDtypeStruct(tuple(dims), dtype)


class Placed:
    def __init__(self, memory_space, dims, dtype=BF):
        self.memory_space, self.shape, self.dtype = memory_space, tuple(dims), jnp.dtype(dtype)
        self.size = functools.reduce(lambda a, b: a * b, self.shape, 1)


SMEM = pltpu.SMEM


def call(kernel, outs, tables, arrays, flops, scratch=()):
    moved = sum(a.size * a.dtype.itemsize for a in arrays) + sum(o.size * o.dtype.itemsize for o in outs)
    places = [o.memory_space if isinstance(o, Placed) else VMEM for o in outs]
    return pl.pallas_call(
        kernel,
        out_shape=tuple(o.memory_space(o.shape, o.dtype) if isinstance(o, Placed) else o for o in outs),
        in_specs=[pl.BlockSpec(memory_space=SMEM)] * len(tables) + [pl.BlockSpec(memory_space=VMEM)] * len(arrays),
        out_specs=tuple(pl.BlockSpec(memory_space=place) for place in places),
        scratch_shapes=list(scratch),
        compiler_params=pltpu.CompilerParams(vmem_limit_bytes=32 * 1024 * 1024),
        cost_estimate=pl.CostEstimate(flops=flops, bytes_accessed=moved, transcendentals=0),
    )(*tables, *arrays)


def dot(a, b):
    return jnp.dot(a, b, preferred_element_type=F32)


def dot_nt(a, b):
    return lax.dot_general(a, b, (((1,), (1,)), ((), ())), preferred_element_type=F32)


def to_rows(wide, count):
    width = wide.shape[1] // count
    return jnp.concatenate([wide[:, j * width : (j + 1) * width] for j in range(count)], axis=0)


def to_lanes(tall, count):
    height = tall.shape[0] // count
    return jnp.concatenate([tall[j * height : (j + 1) * height] for j in range(count)], axis=1)


def gates(preact):
    sigma = 0.5 + 0.5 * jnp.tanh(0.5 * preact)
    hidden = preact * sigma
    return hidden, sigma + hidden * (1.0 - sigma)


def repeat(slots, one):
    if slots <= 16:
        for q in range(slots):
            one(q)
    else:
        pl.loop(0, slots)(one)


def advect(read, count, stencil, cubic_ref):
    parts = [jnp.concatenate([read(t, k) for t in range(count)], axis=0) for k in range(stencil)]
    return to_lanes(dot(jnp.concatenate(parts, axis=1), cubic_ref[...]), count)


def entry_of(sends_ref, section, q):
    cap = sends_ref.shape[2]
    return sends_ref[section, 0, q % cap, q // cap]


def send_terms(ladv, count, stencil, section, slots_ref, cubic_ref, terms_ref, target, sem):
    width = ladv.shape[1] // count
    height = ladv.shape[0]
    terms = dot_nt(to_rows(ladv, count).astype(BF), cubic_ref[...])
    for j in range(count):
        for k in range(stencil):
            block = terms[j * height : (j + 1) * height, k * width : (k + 1) * width]
            terms_ref[j * stencil + k] = block.astype(BF)
            pltpu.make_async_copy(terms_ref.at[j * stencil + k], target(slots_ref[section, j, k]), sem).start()


def collect(sends_ref, section, slots, read, total_ref):
    total_ref[...] = jnp.zeros(total_ref.shape, F32)

    def one(q):
        entry = entry_of(sends_ref, section, q)

        @pl.when(entry >= 0)
        def _():
            total_ref[entry] += read(q).astype(F32)

    repeat(slots, one)


def padded(block, rows):
    block = block.astype(F32)
    return jnp.concatenate([block, jnp.zeros((rows - block.shape[0], block.shape[1]), F32)], axis=0)


def own_kernel(slots_in_ref, sends_in_ref, state_in_ref, out_ref, slots_ref, sends_ref, state_ref, note_ref, sems):
    pairs = ((sends_in_ref, sends_ref), (slots_in_ref, slots_ref), (state_in_ref, state_ref))
    loads = [pltpu.make_async_copy(a, b, sems.at[i]) for i, (a, b) in enumerate(pairs)]
    for load in loads:
        load.start()
    for load in loads:
        load.wait()
    count, channels, _ = state_ref.shape
    rows = out_ref.shape[1]
    note_ref[...] = jnp.zeros(note_ref.shape, F32)
    for section in range(sends_ref.shape[0]):
        note_ref[section : section + 1, : sends_ref.shape[3]] = sends_ref[section, 0].astype(F32)
    note_ref[4 : 4 + count, : slots_ref.shape[2]] = slots_ref[0].astype(F32)
    for j in range(1, count):
        out_ref[j] = padded(state_ref[j], rows).astype(BF)
    out_ref[0] = jnp.concatenate([state_ref[0].astype(F32), note_ref[...]], axis=0).astype(BF)


def own_tangent_kernel(slots_in_ref, sends_in_ref, tangent_in_ref, out_ref, slots_ref, sends_ref, tangent_ref, sems):
    pairs = ((sends_in_ref, sends_ref), (slots_in_ref, slots_ref), (tangent_in_ref, tangent_ref))
    loads = [pltpu.make_async_copy(a, b, sems.at[i]) for i, (a, b) in enumerate(pairs)]
    for load in loads:
        load.start()
    for load in loads:
        load.wait()
    for j in range(tangent_ref.shape[0]):
        out_ref[j] = padded(tangent_ref[j], out_ref.shape[1]).astype(BF)


def prepare_kernel(w_in_t_ref, w_out_ref, cubic_in_ref, cot_ref, w_in_ref, w_out_pad_ref, w_out_t_ref, cubic_ref, lam_ref):
    cubic_ref[...] = cubic_in_ref[...]
    lam_ref[...] = side_by_side(cot_ref)
    rows = w_out_pad_ref.shape[0]
    w_in_ref[...] = padded(w_in_t_ref[...], rows).T.astype(BF)
    w_out_pad_ref[...] = padded(w_out_ref[...], rows).astype(BF)
    w_out_t_ref[...] = w_out_ref[...].astype(F32).T.astype(BF)


def routes(peers, count, stencil, slots_ref, blocks_ref, notes_ref, tables_ref, route_ref, sem):
    me = lax.axis_index("lat")

    def place(device):
        differs = device ^ me
        return (differs & 1) * (peers // 2) + (differs >> 1)

    def read_note(r):
        block = blocks_ref[r * count].astype(F32)
        notes_ref[r] = block[block.shape[0] - notes_ref.shape[1] :].astype(jnp.int32)

    repeat(peers, read_note)
    pltpu.make_async_copy(notes_ref, tables_ref, sem).start()
    pltpu.make_async_copy(notes_ref, tables_ref, sem).wait()

    def fill(t, device, block):
        for k in range(stencil):
            owner = tables_ref[place(device), 4 + block, k]
            entry = jnp.maximum(tables_ref[place(owner), 0, device], 0)
            route_ref[t, k] = place(owner) * count + entry

    for k in range(stencil):
        for j in range(count):
            device = slots_ref[1, j, k]
            fill(k * count + j, device, jnp.maximum(tables_ref[place(device), 1, me], 0))
    for j in range(count):
        fill(stencil * count + j, me, j)


def forward_kernel(peers, count, stencil, slots_ref, blocks_ref, cubic_ref, w_in_ref, w_out_ref, w_in_t_ref, w_out_t_ref, lam_two_ref,
                   send_ref, adv_one_ref, adv_ref, route_ref, notes_ref, tables_ref, terms_ref, sem, note_sem):
    routes(peers, count, stencil, slots_ref, blocks_ref, notes_ref, tables_ref, route_ref, note_sem)
    everyone = (stencil + 1) * count
    adv = advect(lambda t, k: blocks_ref[route_ref[t, k]], everyone, stencil, cubic_ref)
    wide = adv.shape[1] // (stencil + 1)
    columns = wide // count
    adv_one_ref[...] = adv.astype(BF)
    fields = []
    for k in range(stencil):
        part = adv_one_ref[:, k * wide : (k + 1) * wide]
        hidden = gates(dot(w_in_ref[...], part))[0].astype(BF)
        fields.append((part.astype(F32) + dot(w_out_ref[...], hidden)).astype(BF))
    adv = advect(lambda j, k: fields[k][:, j * columns : (j + 1) * columns], count, stencil, cubic_ref).astype(BF)
    adv_ref[...] = adv
    lam = lam_two_ref[...]
    slope = gates(dot(w_in_ref[...], adv))[1]
    ghid = (slope * dot(w_out_t_ref[...], lam)).astype(BF)
    ladv = lam.astype(F32) + dot(w_in_t_ref[...], ghid)
    send_terms(ladv, count, stencil, 1, slots_ref, cubic_ref, terms_ref, lambda q: send_ref.at[q], sem)
    pltpu.make_async_copy(terms_ref, terms_ref, sem).wait()


def tangent_kernel(count, stencil, route_ref, blocks_ref, cubic_ref, w_in_ref, w_out_ref, adv_one_ref, adv_two_ref, out_ref):
    def step(adv, tadv):
        slope = gates(dot(w_in_ref[...], adv))[1]
        thid = (slope * dot(w_in_ref[...], tadv)).astype(BF)
        return tadv.astype(F32) + dot(w_out_ref[...], thid)

    tadv = advect(lambda t, k: blocks_ref[route_ref[t, k]], stencil * count, stencil, cubic_ref).astype(BF)
    wide = tadv.shape[1] // stencil
    columns = wide // count
    fields = []
    for k in range(stencil):
        fields.append(step(adv_one_ref[:, k * wide : (k + 1) * wide], tadv[:, k * wide : (k + 1) * wide]).astype(BF))
    tadv = advect(lambda j, k: fields[k][:, j * columns : (j + 1) * columns], count, stencil, cubic_ref).astype(BF)
    pert = step(adv_two_ref[...], tadv)
    channels = out_ref.shape[1]
    for j in range(count):
        out_ref[j] = pert[:channels, j * columns : (j + 1) * columns].astype(BF)


def side_by_side(ref):
    return jnp.concatenate([ref[j] for j in range(ref.shape[0])], axis=1)


def between_kernel(lam_two_ref, w_in_ref, w_out_t_ref, adv_two_ref, adv_all_ref, in_ref, out_ref, adv_one_ref, hidden_ref, slope_ref):
    lam = lam_two_ref[...]
    channels, wide = lam.shape
    adv = adv_two_ref[...]
    hidden, slope = gates(dot(w_in_ref[...], adv))
    ghid = (slope * dot(w_out_t_ref[...], lam)).astype(BF)
    in_ref[...] = dot_nt(adv, ghid)[:channels]
    out_ref[...] = dot_nt(lam, hidden.astype(BF))
    adv = adv_all_ref[:, adv_all_ref.shape[1] - wide :]
    adv_one_ref[...] = adv
    hidden, slope = gates(dot(w_in_ref[...], adv))
    hidden_ref[...] = hidden.astype(BF)
    slope_ref[...] = slope.astype(BF)


def third_kernel(count, stencil, slots, slots_ref, sends_ref, recv_ref, cubic_ref, w_in_t_ref, w_out_t_ref, slope_ref,
                 send_ref, lam_ref, ghid_ref, total_ref, terms_ref, sem):
    collect(sends_ref, 1, slots, lambda q: recv_ref[q], total_ref)
    lam = side_by_side(total_ref).astype(BF)
    lam_ref[...] = lam
    ghid = (slope_ref[...].astype(F32) * dot(w_out_t_ref[...], lam)).astype(BF)
    ghid_ref[...] = ghid
    ladv = lam.astype(F32) + dot(w_in_t_ref[...], ghid)
    send_terms(ladv, count, stencil, 0, slots_ref, cubic_ref, terms_ref, lambda q: send_ref.at[q], sem)
    pltpu.make_async_copy(terms_ref, terms_ref, sem).wait()


def grad_pair_kernel(side_ref, lam_ref, hidden_ref, ghid_ref, adv_ref, in_ref, out_ref, keep_ref, give_ref):
    grad_in = dot_nt(adv_ref[...], ghid_ref[...])
    grad_in = (in_ref[...] + grad_in[: in_ref.shape[0]]).astype(BF)
    grad_out = (out_ref[...] + dot_nt(lam_ref[...], hidden_ref[...])).astype(BF)

    @pl.when(side_ref[0] == 0)
    def _():
        keep_ref[...] = grad_in
        give_ref[...] = grad_out

    @pl.when(side_ref[0] != 0)
    def _():
        keep_ref[...] = grad_out
        give_ref[...] = grad_in


def last_kernel(slots, sends_ref, recv_ref, back_ref):
    collect(sends_ref, 0, slots, lambda q: recv_ref[q], back_ref)


def shards(state, tangent, cotangent, cubic, w_in, w_out, slots, sends):
    count, channels, columns = state.shape
    stencil = cubic.shape[0]
    hid = w_in.shape[0]
    peers = lax.axis_size("lat")
    slot_count = peers * sends.shape[-1]
    wide = count * columns
    block = (channels, columns)
    blocks = (count, *block)
    side = lax.axis_index("lat") % 2
    sends = jnp.transpose(sends, (0, 1, 3, 2))
    cubic = cubic.reshape(stencil * columns, columns)
    w_in_t = w_in.T
    mix = 2 * wide * channels * stencil * columns
    net = 2 * wide * channels * hid
    sizes = (count, stencil, slot_count)
    sem = pltpu.SemaphoreType.DMA

    def exchange(packed):
        return lax.all_to_all(packed, "lat", split_axis=0, concat_axis=0, tiled=True)

    def swap(values, step):
        return lax.ppermute(values, "lat", [(i, i ^ step) for i in range(peers)])

    def add(a, b):
        return (a.astype(F32) + b.astype(F32)).astype(BF)

    def widen(held, step):
        other = swap(held, step)
        if step == 1:
            return jnp.concatenate([held, other], axis=0)
        return jnp.stack([held, other], axis=1).reshape(-1, *held.shape[1:])

    tie = lax.optimization_barrier

    def load(kernel, arrays, out_shape, scratch):
        return pl.pallas_call(
            kernel,
            out_shape=out_shape,
            in_specs=[pl.BlockSpec(memory_space=HBM)] * len(arrays),
            out_specs=tuple(pl.BlockSpec(memory_space=place) for place in (VMEM, SMEM, SMEM)[: len(out_shape)]),
            scratch_shapes=scratch,
        )(*(pltpu.with_memory_space_constraint(a, HBM) for a in arrays))

    tall = -(-(channels + 4 + count) // 16) * 16
    rest = tall - channels
    (own,) = load(
        own_kernel, (slots, sends, state), (VMEM((count, tall, columns), BF),),
        [VMEM(slots.shape, slots.dtype), VMEM(sends.shape, sends.dtype), VMEM(blocks, BF), VMEM((rest, columns), F32), sem((3,))],
    )
    steps = []
    while 2 ** len(steps) < peers:
        steps.insert(0, 2 ** len(steps))
    states = widen(own[None], steps[0])
    own, slots, sends = load(
        own_tangent_kernel, (slots, sends, tangent),
        (VMEM((count, tall, columns), BF), SMEM(slots.shape, slots.dtype), SMEM(sends.shape, sends.dtype)),
        [VMEM(blocks, BF), sem((3,))],
    )
    w_in, w_out_pad, w_out_t, cubic, lam_two = call(
        prepare_kernel,
        [shape((hid, tall)), shape((tall, hid)), shape((hid, channels)),
         Placed(VMEM, cubic.shape), Placed(VMEM, (channels, wide))],
        [], [w_in_t, w_out, cubic, cotangent], 0,
    )
    tangents = widen(own[None], steps[0])
    states = widen(states, steps[1])
    for i in range(2, len(steps)):
        if i < len(steps) - 1:
            states, tangents = tie((states, tangents))
        else:
            states, tangents, w_in, cubic, lam_two = tie((states, tangents, w_in, cubic, lam_two))
        states = widen(states, steps[i])
        if i < len(steps) - 1:
            tangents = widen(tangents, steps[i - 1])
    states, tangents = tie((states, tangents))
    tangents = widen(tangents, steps[-2])
    states = states.reshape(-1, tall, columns)
    everyone = (stencil + 1) * count
    send, adv_all, adv_two, route = call(
        functools.partial(forward_kernel, peers, count, stencil),
        [Placed(HBM, (slot_count, *block)), shape((tall, everyone * columns)), shape((tall, wide)),
         Placed(SMEM, (everyone, stencil), jnp.int32)],
        [slots], [states, cubic, w_in, w_out_pad, w_in_t, w_out_t, lam_two], 7 * mix + 11 * net,
        [VMEM((peers, rest, columns), jnp.int32), SMEM((peers, rest, columns), jnp.int32),
         VMEM((count * stencil, *block), BF), sem, sem],
    )
    recv_three = exchange(send)
    _, tangents = tie((send, tangents))
    tangents = widen(tangents, 1).reshape(-1, tall, columns)
    part_in, part_out, adv_one, hidden_one, slope_one = call(
        between_kernel,
        [shape((channels, hid), F32)] * 2 + [shape((tall, wide))] + [shape((hid, wide))] * 2,
        [], [lam_two, w_in, w_out_t, adv_two, adv_all], 5 * net,
    )
    (pert,) = call(
        functools.partial(tangent_kernel, count, stencil),
        [shape(blocks)], [route], [tangents, cubic, w_in, w_out_pad, adv_all, adv_two], 5 * mix + 15 * net,
    )
    recv_three, pert = tie((recv_three, pert))
    send, lam_one, ghid_one = call(
        functools.partial(third_kernel, *sizes),
        [Placed(HBM, (slot_count, *block)), shape((channels, wide)), shape((hid, wide))],
        [slots, sends], [recv_three, cubic, w_in_t, w_out_t, slope_one], mix + 2 * net,
        [VMEM(blocks, F32), VMEM((count * stencil, *block), BF), sem],
    )
    recv_four = exchange(send)
    mine, give = call(
        grad_pair_kernel,
        [shape((channels, hid))] * 2, [side.astype(jnp.int32).reshape(1)],
        [lam_one, hidden_one, ghid_one, adv_one, part_in, part_out], 2 * net,
    )
    mine = add(mine, swap(give, 1))
    step = 2
    while step < peers:
        if 2 * step < peers:
            near, far, both = swap(mine, step), swap(mine, 2 * step), swap(mine, 3 * step)
            mine = ((mine.astype(F32) + near.astype(F32)) + (far.astype(F32) + both.astype(F32))).astype(BF)
            step *= 4
        else:
            mine, recv_four, pert = tie((mine, recv_four, pert))
            mine = add(mine, swap(mine, step))
            step *= 2
    (back,) = call(functools.partial(last_kernel, slot_count), [shape(blocks, F32)], [sends], [recv_four], net)
    other = swap(mine, 1)
    grad_in = jnp.where(side == 0, mine, other).astype(F32).T
    grad_out = jnp.where(side == 0, other, mine).astype(F32)
    return (pert, back, grad_in, grad_out)


def solution(mesh):
    in_specs = (
        P(("grp", "lat"), None, None),
        P(("grp", "lat"), None, None),
        P(("grp", "lat"), None, None),
        P(),
        P(),
        P(),
        P("grp", "lat", None),
        P("grp", "lat", None, None),
    )
    out_specs = (
        P(("grp", "lat"), None, None),
        P(("grp", "lat"), None, None),
        P("grp", None),
        P("grp", None),
    )
    return jax.shard_map(shards, mesh=mesh, in_specs=in_specs, out_specs=out_specs, check_vma=False)
```

```python
import functools

import jax
import jax.numpy as jnp
from jax import lax
from jax.experimental import pallas as pl
from jax.experimental.pallas import tpu as pltpu
from jax.sharding import PartitionSpec as P

BF = jnp.bfloat16
F32 = jnp.float32
VMEM = pltpu.VMEM
HBM = pltpu.HBM
LANES = 128


def shape(dims, dtype=BF):
    return jax.ShapeDtypeStruct(tuple(dims), dtype)


class Placed:
    def __init__(self, memory_space, dims, dtype=BF):
        self.memory_space, self.shape, self.dtype = memory_space, tuple(dims), jnp.dtype(dtype)
        self.size = functools.reduce(lambda a, b: a * b, self.shape, 1)


SMEM = pltpu.SMEM


def call(kernel, outs, tables, arrays, flops, scratch=()):
    moved = sum(a.size * a.dtype.itemsize for a in arrays) + sum(o.size * o.dtype.itemsize for o in outs)
    places = [o.memory_space if isinstance(o, Placed) else VMEM for o in outs]
    return pl.pallas_call(
        kernel,
        out_shape=tuple(o.memory_space(o.shape, o.dtype) if isinstance(o, Placed) else o for o in outs),
        in_specs=[pl.BlockSpec(memory_space=SMEM)] * len(tables) + [pl.BlockSpec(memory_space=VMEM)] * len(arrays),
        out_specs=tuple(pl.BlockSpec(memory_space=place) for place in places),
        scratch_shapes=list(scratch),
        compiler_params=pltpu.CompilerParams(vmem_limit_bytes=32 * 1024 * 1024),
        cost_estimate=pl.CostEstimate(flops=flops, bytes_accessed=moved, transcendentals=0),
    )(*tables, *arrays)


def dot(a, b):
    return jnp.dot(a, b, preferred_element_type=F32)


def dot_nt(a, b):
    return lax.dot_general(a, b, (((1,), (1,)), ((), ())), preferred_element_type=F32)


def to_rows(wide, count):
    width = wide.shape[1] // count
    return jnp.concatenate([wide[:, j * width : (j + 1) * width] for j in range(count)], axis=0)


def to_lanes(tall, count):
    height = tall.shape[0] // count
    return jnp.concatenate([tall[j * height : (j + 1) * height] for j in range(count)], axis=1)


def gates(preact):
    sigma = 0.5 + 0.5 * jnp.tanh(0.5 * preact)
    hidden = preact * sigma
    return hidden, sigma + hidden * (1.0 - sigma)


def repeat(slots, one):
    if slots <= 16:
        for q in range(slots):
            one(q)
    else:
        pl.loop(0, slots)(one)


def advect(read, count, stencil, cubic_ref):
    parts = [jnp.concatenate([read(t, k) for t in range(count)], axis=0) for k in range(stencil)]
    return to_lanes(dot(jnp.concatenate(parts, axis=1), cubic_ref[...]), count)


def entry_of(sends_ref, section, q):
    cap = sends_ref.shape[2]
    return sends_ref[section, 0, q % cap, q // cap]


def send_terms(ladv, count, stencil, section, slots_ref, cubic_ref, terms_ref, target, sem):
    width = ladv.shape[1] // count
    height = ladv.shape[0]
    terms = dot_nt(to_rows(ladv, count).astype(BF), cubic_ref[...])
    for j in range(count):
        for k in range(stencil):
            block = terms[j * height : (j + 1) * height, k * width : (k + 1) * width]
            terms_ref[j * stencil + k] = block.astype(BF)
            pltpu.make_async_copy(terms_ref.at[j * stencil + k], target(slots_ref[section, j, k]), sem).start()


def collect(sends_ref, section, slots, read, total_ref):
    total_ref[...] = jnp.zeros(total_ref.shape, F32)

    def one(q):
        entry = entry_of(sends_ref, section, q)

        @pl.when(entry >= 0)
        def _():
            total_ref[entry] += read(q).astype(F32)

    repeat(slots, one)


def padded(block, rows):
    block = block.astype(F32)
    if rows == block.shape[0]:
        return block
    return jnp.concatenate([block, jnp.zeros((rows - block.shape[0], block.shape[1]), F32)], axis=0)


def own_kernel(slots_in_ref, sends_in_ref, state_in_ref, out_ref, slots_ref, sends_ref, state_ref, note_ref, sems):
    pairs = ((sends_in_ref, sends_ref), (slots_in_ref, slots_ref), (state_in_ref, state_ref))
    loads = [pltpu.make_async_copy(a, b, sems.at[i]) for i, (a, b) in enumerate(pairs)]
    for load in loads:
        load.start()
    for load in loads:
        load.wait()
    count = state_ref.shape[0]
    rows = out_ref.shape[1]
    notes = [jnp.zeros((1, LANES), F32) for _ in range(-(-(2 * sends_ref.shape[3] + slots_ref[0].size) // LANES))]
    peers, reach = sends_ref.shape[3], slots_ref.shape[2]
    numbers = [(section * peers, sends_ref[section, 0]) for section in range(sends_ref.shape[0])]
    numbers += [(2 * peers + j * reach, slots_ref[0, j : j + 1]) for j in range(count)]
    for start, row in numbers:
        row = row.astype(F32)
        if row.shape[1] < LANES:
            row = jnp.concatenate([row, jnp.zeros((1, LANES - row.shape[1]), F32)], axis=1)
        if start % LANES:
            row = pltpu.roll(row, start % LANES, 1)
        notes[start // LANES] += row
    note_ref[...] = jnp.zeros(note_ref.shape, F32)
    for i, row in enumerate(notes):
        note_ref[i : i + 1] = row
    for j in range(1, count):
        out_ref[j] = padded(state_ref[j], rows).astype(BF)
    top = padded(state_ref[0], rows - 8)
    out_ref[0] = jnp.concatenate([top, note_ref[...]], axis=0).astype(BF)


def own_tangent_kernel(slots_in_ref, sends_in_ref, tangent_in_ref, out_ref, slots_ref, sends_ref, tangent_ref, sems):
    pairs = ((sends_in_ref, sends_ref), (slots_in_ref, slots_ref), (tangent_in_ref, tangent_ref))
    loads = [pltpu.make_async_copy(a, b, sems.at[i]) for i, (a, b) in enumerate(pairs)]
    for load in loads:
        load.start()
    for load in loads:
        load.wait()
    for j in range(tangent_ref.shape[0]):
        out_ref[j] = padded(tangent_ref[j], out_ref.shape[1]).astype(BF)


def prepare_kernel(w_in_t_ref, w_out_ref, cubic_in_ref, cot_ref, w_in_ref, w_out_pad_ref, w_out_t_ref, cubic_ref, lam_ref):
    cubic_ref[...] = cubic_in_ref[...]
    lam_ref[...] = side_by_side(cot_ref)
    rows = w_out_pad_ref.shape[0]
    w_in_ref[...] = padded(w_in_t_ref[...], rows).T.astype(BF)
    w_out_pad_ref[...] = padded(w_out_ref[...], rows).astype(BF)
    w_out_t_ref[...] = w_out_ref[...].astype(F32).T.astype(BF)


def routes(peers, count, stencil, slots_ref, blocks_ref, notes_ref, tables_ref, route_ref, sem, meanwhile):
    me = lax.axis_index("lat")
    rows = notes_ref.shape[0] // peers
    under = blocks_ref.shape[1] - 8

    def place(device):
        differs = device ^ me
        return (differs & 1) * (peers // 2) + ((differs >> 1) & 3) * (peers // 8) + (differs >> 3)

    def read_note(r):
        block = blocks_ref[r * count].astype(F32)
        notes_ref[pl.ds(r * rows, rows)] = block[under : under + rows].astype(jnp.int32)

    repeat(peers, read_note)
    copy = pltpu.make_async_copy(notes_ref, tables_ref, sem)
    copy.start()
    meanwhile()
    copy.wait()

    def note(device, start, index):
        return tables_ref[place(device) * rows + start // LANES, start % LANES + index]

    def fill(t, device, block):
        for k in range(stencil):
            owner = note(device, 2 * peers, block * stencil + k)
            entry = jnp.maximum(note(owner, 0, device), 0)
            route_ref[t, k] = place(owner) * count + entry

    for k in range(stencil):
        for j in range(count):
            device = slots_ref[1, j, k]
            fill(k * count + j, device, jnp.maximum(note(device, peers, me), 0))
    for j in range(count):
        fill(stencil * count + j, me, j)


def forward_kernel(peers, count, stencil, slots_ref, blocks_ref, cubic_ref, w_in_ref, w_out_ref, w_in_t_ref, w_out_t_ref, lam_two_ref,
                   send_ref, adv_one_ref, adv_ref, route_ref, notes_ref, tables_ref, terms_ref, pull_ref, sem, note_sem):
    def pull():
        pull_ref[...] = dot(w_out_t_ref[...], lam_two_ref[...])

    routes(peers, count, stencil, slots_ref, blocks_ref, notes_ref, tables_ref, route_ref, note_sem, pull)
    everyone = (stencil + 1) * count
    adv = advect(lambda t, k: blocks_ref[route_ref[t, k]], everyone, stencil, cubic_ref)
    wide = adv.shape[1] // (stencil + 1)
    columns = wide // count
    adv_one_ref[...] = adv.astype(BF)
    fields = []
    for k in range(stencil):
        part = adv_one_ref[:, k * wide : (k + 1) * wide]
        hidden = gates(dot(w_in_ref[...], part))[0].astype(BF)
        fields.append((part.astype(F32) + dot(w_out_ref[...], hidden)).astype(BF))
    adv = advect(lambda j, k: fields[k][:, j * columns : (j + 1) * columns], count, stencil, cubic_ref).astype(BF)
    adv_ref[...] = adv
    lam = lam_two_ref[...]
    slope = gates(dot(w_in_ref[...], adv))[1]
    ghid = (slope * pull_ref[...]).astype(BF)
    ladv = lam.astype(F32) + dot(w_in_t_ref[...], ghid)
    send_terms(ladv, count, stencil, 1, slots_ref, cubic_ref, terms_ref, lambda q: send_ref.at[q], sem)
    pltpu.make_async_copy(terms_ref, terms_ref, sem).wait()


def tangent_kernel(count, stencil, route_ref, blocks_ref, cubic_ref, w_in_ref, w_out_ref, adv_one_ref, adv_two_ref, out_ref):
    def step(adv, tadv):
        slope = gates(dot(w_in_ref[...], adv))[1]
        thid = (slope * dot(w_in_ref[...], tadv)).astype(BF)
        return tadv.astype(F32) + dot(w_out_ref[...], thid)

    tadv = advect(lambda t, k: blocks_ref[route_ref[t, k]], stencil * count, stencil, cubic_ref).astype(BF)
    wide = tadv.shape[1] // stencil
    columns = wide // count
    fields = []
    for k in range(stencil):
        fields.append(step(adv_one_ref[:, k * wide : (k + 1) * wide], tadv[:, k * wide : (k + 1) * wide]).astype(BF))
    tadv = advect(lambda j, k: fields[k][:, j * columns : (j + 1) * columns], count, stencil, cubic_ref).astype(BF)
    pert = step(adv_two_ref[...], tadv)
    channels = out_ref.shape[1]
    for j in range(count):
        out_ref[j] = pert[:channels, j * columns : (j + 1) * columns].astype(BF)


def side_by_side(ref):
    return jnp.concatenate([ref[j] for j in range(ref.shape[0])], axis=1)


def between_kernel(lam_two_ref, w_in_ref, w_out_t_ref, adv_two_ref, adv_all_ref, in_ref, out_ref, adv_one_ref, hidden_ref, slope_ref):
    lam = lam_two_ref[...]
    channels, wide = lam.shape
    adv = adv_two_ref[...]
    hidden, slope = gates(dot(w_in_ref[...], adv))
    ghid = (slope * dot(w_out_t_ref[...], lam)).astype(BF)
    in_ref[...] = dot_nt(adv, ghid)[:channels]
    out_ref[...] = dot_nt(lam, hidden.astype(BF))
    adv = adv_all_ref[:, adv_all_ref.shape[1] - wide :]
    adv_one_ref[...] = adv
    hidden, slope = gates(dot(w_in_ref[...], adv))
    hidden_ref[...] = hidden.astype(BF)
    slope_ref[...] = slope.astype(BF)


def third_kernel(count, stencil, slots, slots_ref, sends_ref, recv_ref, cubic_ref, w_in_t_ref, w_out_t_ref, slope_ref,
                 send_ref, lam_ref, ghid_ref, total_ref, terms_ref, sem):
    collect(sends_ref, 1, slots, lambda q: recv_ref[q], total_ref)
    lam = side_by_side(total_ref).astype(BF)
    lam_ref[...] = lam
    ghid = (slope_ref[...].astype(F32) * dot(w_out_t_ref[...], lam)).astype(BF)
    ghid_ref[...] = ghid
    ladv = lam.astype(F32) + dot(w_in_t_ref[...], ghid)
    send_terms(ladv, count, stencil, 0, slots_ref, cubic_ref, terms_ref, lambda q: send_ref.at[q], sem)
    pltpu.make_async_copy(terms_ref, terms_ref, sem).wait()


def grad_pair_kernel(side_ref, lam_ref, hidden_ref, ghid_ref, adv_ref, in_ref, out_ref, keep_ref, give_ref):
    grad_in = dot_nt(adv_ref[...], ghid_ref[...])
    grad_in = (in_ref[...] + grad_in[: in_ref.shape[0]]).astype(BF)
    grad_out = (out_ref[...] + dot_nt(lam_ref[...], hidden_ref[...])).astype(BF)

    @pl.when(side_ref[0] == 0)
    def _():
        keep_ref[...] = grad_in
        give_ref[...] = grad_out

    @pl.when(side_ref[0] != 0)
    def _():
        keep_ref[...] = grad_out
        give_ref[...] = grad_in


def last_kernel(slots, sends_ref, recv_ref, back_ref):
    collect(sends_ref, 0, slots, lambda q: recv_ref[q], back_ref)


def shards(state, tangent, cotangent, cubic, w_in, w_out, slots, sends):
    count, channels, columns = state.shape
    stencil = cubic.shape[0]
    hid = w_in.shape[0]
    peers = lax.axis_size("lat")
    slot_count = peers * sends.shape[-1]
    wide = count * columns
    block = (channels, columns)
    blocks = (count, *block)
    side = lax.axis_index("lat") % 2
    sends = jnp.transpose(sends, (0, 1, 3, 2))
    cubic = cubic.reshape(stencil * columns, columns)
    w_in_t = w_in.T
    mix = 2 * wide * channels * stencil * columns
    net = 2 * wide * channels * hid
    sizes = (count, stencil, slot_count)
    sem = pltpu.SemaphoreType.DMA

    def exchange(packed):
        return lax.all_to_all(packed, "lat", split_axis=0, concat_axis=0, tiled=True)

    def swap(values, step):
        return lax.ppermute(values, "lat", [(i, i ^ step) for i in range(peers)])

    def add(a, b):
        return (a.astype(F32) + b.astype(F32)).astype(BF)

    def widen(held, step):
        return jnp.stack([held, swap(held, step)], axis=1).reshape(-1, *held.shape[1:])

    def cross(near, far):
        half = near.shape[0] // 2
        return swap(far[:half], 2), swap(near[half:], 4)

    tie = lax.optimization_barrier

    def load(kernel, arrays, out_shape, scratch):
        return pl.pallas_call(
            kernel,
            out_shape=out_shape,
            in_specs=[pl.BlockSpec(memory_space=HBM)] * len(arrays),
            out_specs=tuple(pl.BlockSpec(memory_space=place) for place in (VMEM, SMEM, SMEM)[: len(out_shape)]),
            scratch_shapes=scratch,
        )(*(pltpu.with_memory_space_constraint(a, HBM) for a in arrays))

    tall = -(-(channels + 8) // 16) * 16
    note_rows = -(-(2 * peers + count * stencil) // LANES)
    notes = (peers * note_rows, LANES)
    (own,) = load(
        own_kernel, (slots, sends, state), (VMEM((count, tall, columns), BF),),
        [VMEM(slots.shape, slots.dtype), VMEM(sends.shape, sends.dtype), VMEM(blocks, BF), VMEM((8, LANES), F32), sem((3,))],
    )
    steps = []
    while 16 * 2 ** len(steps) <= peers:
        steps.insert(0, 8 * 2 ** len(steps))
    states = own[None]
    for step in steps:
        states = widen(states, step)
    near, far = swap(states, 2), swap(states, 4)
    own, slots, sends = load(
        own_tangent_kernel, (slots, sends, tangent),
        (VMEM((count, tall, columns), BF), SMEM(slots.shape, slots.dtype), SMEM(sends.shape, sends.dtype)),
        [VMEM(blocks, BF), sem((3,))],
    )
    w_in, w_out_pad, w_out_t, cubic, lam_two = call(
        prepare_kernel,
        [shape((hid, tall)), shape((tall, hid)), shape((hid, channels)),
         Placed(VMEM, cubic.shape), Placed(VMEM, (channels, wide))],
        [], [w_in_t, w_out, cubic, cotangent], 0,
    )
    tangents = own[None]
    for step in steps:
        tangents = widen(tangents, step)
    near, far, tangents = tie((near, far, tangents))
    states = jnp.concatenate([states, near, far, *cross(near, far)], axis=0)
    near, far = swap(tangents, 2), swap(tangents, 4)
    states, near, far, w_in, cubic, lam_two = tie((states, near, far, w_in, cubic, lam_two))
    states = jnp.concatenate([states, swap(states, 1)], axis=0)
    states, near, far = tie((states, near, far))
    tangents = jnp.concatenate([tangents, near, far, *cross(near, far)], axis=0)
    states = states.reshape(-1, tall, columns)
    everyone = (stencil + 1) * count
    send, adv_all, adv_two, route = call(
        functools.partial(forward_kernel, peers, count, stencil),
        [Placed(HBM, (slot_count, *block)), shape((tall, everyone * columns)), shape((tall, wide)),
         Placed(SMEM, (everyone, stencil), jnp.int32)],
        [slots], [states, cubic, w_in, w_out_pad, w_in_t, w_out_t, lam_two], 7 * mix + 11 * net,
        [VMEM(notes, jnp.int32), SMEM(notes, jnp.int32), VMEM((count * stencil, *block), BF), VMEM((hid, wide), F32), sem, sem],
    )
    recv_three = exchange(send)
    _, tangents = tie((send, tangents))
    tangents = jnp.concatenate([tangents, swap(tangents, 1)], axis=0).reshape(-1, tall, columns)
    part_in, part_out, adv_one, hidden_one, slope_one = call(
        between_kernel,
        [shape((channels, hid), F32)] * 2 + [shape((tall, wide))] + [shape((hid, wide))] * 2,
        [], [lam_two, w_in, w_out_t, adv_two, adv_all], 5 * net,
    )
    (pert,) = call(
        functools.partial(tangent_kernel, count, stencil),
        [shape(blocks)], [route], [tangents, cubic, w_in, w_out_pad, adv_all, adv_two], 5 * mix + 15 * net,
    )
    recv_three, pert = tie((recv_three, pert))
    send, lam_one, ghid_one = call(
        functools.partial(third_kernel, *sizes),
        [Placed(HBM, (slot_count, *block)), shape((channels, wide)), shape((hid, wide))],
        [slots, sends], [recv_three, cubic, w_in_t, w_out_t, slope_one], mix + 2 * net,
        [VMEM(blocks, F32), VMEM((count * stencil, *block), BF), sem],
    )
    recv_four = exchange(send)
    mine, give = call(
        grad_pair_kernel,
        [shape((channels, hid))] * 2, [side.astype(jnp.int32).reshape(1)],
        [lam_one, hidden_one, ghid_one, adv_one, part_in, part_out], 2 * net,
    )
    mine = add(mine, swap(give, 1))
    step = peers // 2
    if len(steps) % 2:
        mine = add(mine, swap(mine, step))
        step //= 2
    while step > 1:
        near, far, both = swap(mine, step // 2), swap(mine, step), swap(mine, step // 2 * 3)
        mine = ((mine.astype(F32) + near.astype(F32)) + (far.astype(F32) + both.astype(F32))).astype(BF)
        step //= 4
    mine, recv_four = tie((mine, recv_four))
    (back,) = call(functools.partial(last_kernel, slot_count), [shape(blocks, F32)], [sends], [recv_four], net)
    other = swap(mine, 1)
    grad_in = jnp.where(side == 0, mine, other).astype(F32).T
    grad_out = jnp.where(side == 0, other, mine).astype(F32)
    return (pert, back, grad_in, grad_out)


def solution(mesh):
    in_specs = (
        P(("grp", "lat"), None, None),
        P(("grp", "lat"), None, None),
        P(("grp", "lat"), None, None),
        P(),
        P(),
        P(),
        P("grp", "lat", None),
        P("grp", "lat", None, None),
    )
    out_specs = (
        P(("grp", "lat"), None, None),
        P(("grp", "lat"), None, None),
        P("grp", None),
        P("grp", None),
    )
    return jax.shard_map(shards, mesh=mesh, in_specs=in_specs, out_specs=out_specs, check_vma=False)
```

```python
import functools

import jax
import jax.numpy as jnp
from jax import lax
from jax.experimental import pallas as pl
from jax.experimental.pallas import tpu as pltpu
from jax.sharding import PartitionSpec as P

BF = jnp.bfloat16
F32 = jnp.float32
VMEM = pltpu.VMEM
HBM = pltpu.HBM
LANES = 128


def shape(dims, dtype=BF):
    return jax.ShapeDtypeStruct(tuple(dims), dtype)


class Placed:
    def __init__(self, memory_space, dims, dtype=BF):
        self.memory_space, self.shape, self.dtype = memory_space, tuple(dims), jnp.dtype(dtype)
        self.size = functools.reduce(lambda a, b: a * b, self.shape, 1)


SMEM = pltpu.SMEM


def call(kernel, outs, tables, arrays, flops, scratch=()):
    moved = sum(a.size * a.dtype.itemsize for a in arrays) + sum(o.size * o.dtype.itemsize for o in outs)
    places = [o.memory_space if isinstance(o, Placed) else VMEM for o in outs]
    return pl.pallas_call(
        kernel,
        out_shape=tuple(o.memory_space(o.shape, o.dtype) if isinstance(o, Placed) else o for o in outs),
        in_specs=[pl.BlockSpec(memory_space=SMEM)] * len(tables) + [pl.BlockSpec(memory_space=VMEM)] * len(arrays),
        out_specs=tuple(pl.BlockSpec(memory_space=place) for place in places),
        scratch_shapes=list(scratch),
        compiler_params=pltpu.CompilerParams(vmem_limit_bytes=32 * 1024 * 1024),
        cost_estimate=pl.CostEstimate(flops=flops, bytes_accessed=moved, transcendentals=0),
    )(*tables, *arrays)


def dot(a, b):
    return jnp.dot(a, b, preferred_element_type=F32)


def dot_nt(a, b):
    return lax.dot_general(a, b, (((1,), (1,)), ((), ())), preferred_element_type=F32)


def to_rows(wide, count):
    width = wide.shape[1] // count
    return jnp.concatenate([wide[:, j * width : (j + 1) * width] for j in range(count)], axis=0)


def to_lanes(tall, count):
    height = tall.shape[0] // count
    return jnp.concatenate([tall[j * height : (j + 1) * height] for j in range(count)], axis=1)


def gates(preact):
    sigma = 0.5 + 0.5 * jnp.tanh(0.5 * preact)
    hidden = preact * sigma
    return hidden, sigma + hidden * (1.0 - sigma)


def repeat(slots, one):
    if slots <= 16:
        for q in range(slots):
            one(q)
    else:
        pl.loop(0, slots)(one)


def advect(read, count, stencil, cubic_ref):
    parts = [jnp.concatenate([read(t, k) for t in range(count)], axis=0) for k in range(stencil)]
    return to_lanes(dot(jnp.concatenate(parts, axis=1), cubic_ref[...]), count)


def entry_of(sends_ref, section, q):
    cap = sends_ref.shape[2]
    return sends_ref[section, 0, q % cap, q // cap]


def send_terms(ladv, count, stencil, section, slots_ref, cubic_ref, terms_ref, target, sem):
    width = ladv.shape[1] // count
    height = ladv.shape[0]
    terms = dot_nt(to_rows(ladv, count).astype(BF), cubic_ref[...])
    for j in range(count):
        for k in range(stencil):
            block = terms[j * height : (j + 1) * height, k * width : (k + 1) * width]
            terms_ref[j * stencil + k] = block.astype(BF)
            pltpu.make_async_copy(terms_ref.at[j * stencil + k], target(slots_ref[section, j, k]), sem).start()


def collect(sends_ref, section, slots, read, total_ref):
    total_ref[...] = jnp.zeros(total_ref.shape, F32)

    def one(q):
        entry = entry_of(sends_ref, section, q)

        @pl.when(entry >= 0)
        def _():
            total_ref[entry] += read(q).astype(F32)

    repeat(slots, one)


def padded(block, rows):
    block = block.astype(F32)
    if rows == block.shape[0]:
        return block
    return jnp.concatenate([block, jnp.zeros((rows - block.shape[0], block.shape[1]), F32)], axis=0)


def own_kernel(slots_in_ref, sends_in_ref, state_in_ref, out_ref, slots_ref, sends_ref, state_ref, note_ref, sems):
    pairs = ((sends_in_ref, sends_ref), (slots_in_ref, slots_ref), (state_in_ref, state_ref))
    loads = [pltpu.make_async_copy(a, b, sems.at[i]) for i, (a, b) in enumerate(pairs)]
    for load in loads:
        load.start()
    for load in loads:
        load.wait()
    count = state_ref.shape[0]
    rows = out_ref.shape[1]
    notes = [jnp.zeros((1, LANES), F32) for _ in range(-(-(2 * sends_ref.shape[3] + slots_ref[0].size) // LANES))]
    peers, reach = sends_ref.shape[3], slots_ref.shape[2]
    numbers = [(section * peers, sends_ref[section, 0]) for section in range(sends_ref.shape[0])]
    numbers += [(2 * peers + j * reach, slots_ref[0, j : j + 1]) for j in range(count)]
    for start, row in numbers:
        row = row.astype(F32)
        if row.shape[1] < LANES:
            row = jnp.concatenate([row, jnp.zeros((1, LANES - row.shape[1]), F32)], axis=1)
        if start % LANES:
            row = pltpu.roll(row, start % LANES, 1)
        notes[start // LANES] += row
    note_ref[...] = jnp.zeros(note_ref.shape, F32)
    for i, row in enumerate(notes):
        note_ref[i : i + 1] = row
    for j in range(1, count):
        out_ref[j] = padded(state_ref[j], rows).astype(BF)
    top = padded(state_ref[0], rows - 8)
    out_ref[0] = jnp.concatenate([top, note_ref[...]], axis=0).astype(BF)


def own_tangent_kernel(slots_in_ref, sends_in_ref, tangent_in_ref, out_ref, slots_ref, sends_ref, tangent_ref, sems):
    pairs = ((sends_in_ref, sends_ref), (slots_in_ref, slots_ref), (tangent_in_ref, tangent_ref))
    loads = [pltpu.make_async_copy(a, b, sems.at[i]) for i, (a, b) in enumerate(pairs)]
    for load in loads:
        load.start()
    for load in loads:
        load.wait()
    for j in range(tangent_ref.shape[0]):
        out_ref[j] = padded(tangent_ref[j], out_ref.shape[1]).astype(BF)


def prepare_kernel(w_in_t_hbm, w_out_hbm, cubic_hbm, cot_hbm, w_in_ref, w_out_pad_ref, w_out_t_ref, cubic_ref, lam_ref,
                   w_in_t_ref, w_out_ref, cot_ref, sems):
    pairs = ((w_in_t_hbm, w_in_t_ref), (w_out_hbm, w_out_ref), (cot_hbm, cot_ref), (cubic_hbm, cubic_ref))
    loads = [pltpu.make_async_copy(a, b, sems.at[i]) for i, (a, b) in enumerate(pairs)]
    for load in loads:
        load.start()
    for load in loads:
        load.wait()
    lam_ref[...] = side_by_side(cot_ref)
    rows = w_out_pad_ref.shape[0]
    w_in_ref[...] = padded(w_in_t_ref[...], rows).T.astype(BF)
    w_out_pad_ref[...] = padded(w_out_ref[...], rows).astype(BF)
    w_out_t_ref[...] = w_out_ref[...].astype(F32).T.astype(BF)


def routes(peers, count, stencil, slots_ref, blocks_ref, notes_ref, tables_ref, route_ref, sem, meanwhile):
    me = lax.axis_index("lat")
    rows = notes_ref.shape[0] // peers
    under = blocks_ref.shape[1] - 8

    def place(device):
        differs = device ^ me
        return (differs & 1) * (peers // 2) + ((differs >> 1) & 3) * (peers // 8) + (differs >> 3)

    def read_note(r):
        block = blocks_ref[r * count].astype(F32)
        notes_ref[pl.ds(r * rows, rows)] = block[under : under + rows].astype(jnp.int32)

    repeat(peers, read_note)
    copy = pltpu.make_async_copy(notes_ref, tables_ref, sem)
    copy.start()
    meanwhile()
    copy.wait()

    def note(device, start, index):
        return tables_ref[place(device) * rows + start // LANES, start % LANES + index]

    def fill(t, device, block):
        for k in range(stencil):
            owner = note(device, 2 * peers, block * stencil + k)
            entry = jnp.maximum(note(owner, 0, device), 0)
            route_ref[t, k] = place(owner) * count + entry

    for k in range(stencil):
        for j in range(count):
            device = slots_ref[1, j, k]
            fill(k * count + j, device, jnp.maximum(note(device, peers, me), 0))
    for j in range(count):
        fill(stencil * count + j, me, j)


def forward_kernel(peers, count, stencil, slots_ref, blocks_ref, cubic_ref, w_in_ref, w_out_ref, w_in_t_ref, w_out_t_ref, lam_two_ref,
                   send_ref, adv_one_ref, adv_ref, route_ref, notes_ref, tables_ref, terms_ref, pull_ref, sem, note_sem):
    def pull():
        pull_ref[...] = dot(w_out_t_ref[...], lam_two_ref[...])

    routes(peers, count, stencil, slots_ref, blocks_ref, notes_ref, tables_ref, route_ref, note_sem, pull)
    everyone = (stencil + 1) * count
    adv = advect(lambda t, k: blocks_ref[route_ref[t, k]], everyone, stencil, cubic_ref)
    wide = adv.shape[1] // (stencil + 1)
    columns = wide // count
    adv_one_ref[...] = adv.astype(BF)
    fields = []
    for k in range(stencil):
        part = adv_one_ref[:, k * wide : (k + 1) * wide]
        hidden = gates(dot(w_in_ref[...], part))[0].astype(BF)
        fields.append((part.astype(F32) + dot(w_out_ref[...], hidden)).astype(BF))
    adv = advect(lambda j, k: fields[k][:, j * columns : (j + 1) * columns], count, stencil, cubic_ref).astype(BF)
    adv_ref[...] = adv
    lam = lam_two_ref[...]
    slope = gates(dot(w_in_ref[...], adv))[1]
    ghid = (slope * pull_ref[...]).astype(BF)
    ladv = lam.astype(F32) + dot(w_in_t_ref[...], ghid)
    send_terms(ladv, count, stencil, 1, slots_ref, cubic_ref, terms_ref, lambda q: send_ref.at[q], sem)
    pltpu.make_async_copy(terms_ref, terms_ref, sem).wait()


def tangent_kernel(count, stencil, route_ref, blocks_ref, cubic_ref, w_in_ref, w_out_ref, adv_one_ref, adv_two_ref, out_ref):
    def step(adv, tadv):
        slope = gates(dot(w_in_ref[...], adv))[1]
        thid = (slope * dot(w_in_ref[...], tadv)).astype(BF)
        return tadv.astype(F32) + dot(w_out_ref[...], thid)

    tadv = advect(lambda t, k: blocks_ref[route_ref[t, k]], stencil * count, stencil, cubic_ref).astype(BF)
    wide = tadv.shape[1] // stencil
    columns = wide // count
    fields = []
    for k in range(stencil):
        fields.append(step(adv_one_ref[:, k * wide : (k + 1) * wide], tadv[:, k * wide : (k + 1) * wide]).astype(BF))
    tadv = advect(lambda j, k: fields[k][:, j * columns : (j + 1) * columns], count, stencil, cubic_ref).astype(BF)
    pert = step(adv_two_ref[...], tadv)
    channels = out_ref.shape[1]
    for j in range(count):
        out_ref[j] = pert[:channels, j * columns : (j + 1) * columns].astype(BF)


def side_by_side(ref):
    return jnp.concatenate([ref[j] for j in range(ref.shape[0])], axis=1)


def between_kernel(lam_two_ref, w_in_ref, w_out_t_ref, adv_two_ref, adv_all_ref, in_ref, out_ref, adv_one_ref, hidden_ref, slope_ref):
    lam = lam_two_ref[...]
    channels, wide = lam.shape
    adv = adv_two_ref[...]
    hidden, slope = gates(dot(w_in_ref[...], adv))
    ghid = (slope * dot(w_out_t_ref[...], lam)).astype(BF)
    in_ref[...] = dot_nt(adv, ghid)[:channels]
    out_ref[...] = dot_nt(lam, hidden.astype(BF))
    adv = adv_all_ref[:, adv_all_ref.shape[1] - wide :]
    adv_one_ref[...] = adv
    hidden, slope = gates(dot(w_in_ref[...], adv))
    hidden_ref[...] = hidden.astype(BF)
    slope_ref[...] = slope.astype(BF)


def third_kernel(count, stencil, slots, slots_ref, sends_ref, recv_ref, cubic_ref, w_in_t_ref, w_out_t_ref, slope_ref,
                 hidden_ref, adv_ref, part_in_ref, part_out_ref, send_ref, keep_ref, give_ref, total_ref, terms_ref, sem):
    collect(sends_ref, 1, slots, lambda q: recv_ref[q], total_ref)
    lam = side_by_side(total_ref).astype(BF)
    ghid = (slope_ref[...].astype(F32) * dot(w_out_t_ref[...], lam)).astype(BF)
    ladv = lam.astype(F32) + dot(w_in_t_ref[...], ghid)
    send_terms(ladv, count, stencil, 0, slots_ref, cubic_ref, terms_ref, lambda q: send_ref.at[q], sem)
    grad_in = dot_nt(adv_ref[...], ghid)
    grad_in = (part_in_ref[...] + grad_in[: part_in_ref.shape[0]]).astype(BF)
    grad_out = (part_out_ref[...] + dot_nt(lam, hidden_ref[...])).astype(BF)
    side = lax.axis_index("lat") & 1

    @pl.when(side == 0)
    def _():
        keep_ref[...] = grad_in
        give_ref[...] = grad_out

    @pl.when(side != 0)
    def _():
        keep_ref[...] = grad_out
        give_ref[...] = grad_in

    pltpu.make_async_copy(terms_ref, terms_ref, sem).wait()


def last_kernel(slots, sends_ref, recv_ref, back_ref):
    collect(sends_ref, 0, slots, lambda q: recv_ref[q], back_ref)


def shards(state, tangent, cotangent, cubic, w_in, w_out, slots, sends):
    count, channels, columns = state.shape
    stencil = cubic.shape[0]
    hid = w_in.shape[0]
    peers = lax.axis_size("lat")
    slot_count = peers * sends.shape[-1]
    wide = count * columns
    block = (channels, columns)
    blocks = (count, *block)
    side = lax.axis_index("lat") % 2
    sends = jnp.transpose(sends, (0, 1, 3, 2))
    cubic = cubic.reshape(stencil * columns, columns)
    w_in_t = w_in.T
    mix = 2 * wide * channels * stencil * columns
    net = 2 * wide * channels * hid
    sizes = (count, stencil, slot_count)
    sem = pltpu.SemaphoreType.DMA

    def exchange(packed):
        return lax.all_to_all(packed, "lat", split_axis=0, concat_axis=0, tiled=True)

    def swap(values, step):
        return lax.ppermute(values, "lat", [(i, i ^ step) for i in range(peers)])

    def add(a, b):
        return (a.astype(F32) + b.astype(F32)).astype(BF)

    def widen(held, step):
        return jnp.stack([held, swap(held, step)], axis=1).reshape(-1, *held.shape[1:])

    def cross(near, far):
        half = near.shape[0] // 2
        return swap(far[:half], 2), swap(near[half:], 4)

    tie = lax.optimization_barrier

    def load(kernel, arrays, out_shape, scratch):
        return pl.pallas_call(
            kernel,
            out_shape=out_shape,
            in_specs=[pl.BlockSpec(memory_space=HBM)] * len(arrays),
            out_specs=tuple(pl.BlockSpec(memory_space=o.memory_space) for o in out_shape),
            scratch_shapes=scratch,
        )(*(pltpu.with_memory_space_constraint(a, HBM) for a in arrays))

    tall = -(-(channels + 8) // 16) * 16
    note_rows = -(-(2 * peers + count * stencil) // LANES)
    notes = (peers * note_rows, LANES)
    (own,) = load(
        own_kernel, (slots, sends, state), (VMEM((count, tall, columns), BF),),
        [VMEM(slots.shape, slots.dtype), VMEM(sends.shape, sends.dtype), VMEM(blocks, BF), VMEM((8, LANES), F32), sem((3,))],
    )
    steps = []
    while 16 * 2 ** len(steps) <= peers:
        steps.insert(0, 8 * 2 ** len(steps))
    states = own[None]
    for step in steps:
        states = widen(states, step)
    near, far = swap(states, 2), swap(states, 4)
    own, slots, sends = load(
        own_tangent_kernel, (slots, sends, tangent),
        (VMEM((count, tall, columns), BF), SMEM(slots.shape, slots.dtype), SMEM(sends.shape, sends.dtype)),
        [VMEM(blocks, BF), sem((3,))],
    )
    w_in, w_out_pad, w_out_t, cubic, lam_two = load(
        prepare_kernel, (w_in_t, w_out, cubic, cotangent),
        tuple(VMEM(dims, BF) for dims in ((hid, tall), (tall, hid), (hid, channels), cubic.shape, (channels, wide))),
        [VMEM(w_in_t.shape, BF), VMEM(w_out.shape, BF), VMEM(blocks, BF), sem((4,))],
    )
    tangents = own[None]
    for step in steps:
        tangents = widen(tangents, step)
    near, far, tangents = tie((near, far, tangents))
    states = jnp.concatenate([states, near, far, *cross(near, far)], axis=0)
    near, far = swap(tangents, 2), swap(tangents, 4)
    states, w_in, cubic, lam_two = tie((states, w_in, cubic, lam_two))
    states = jnp.concatenate([states, swap(states, 1)], axis=0)
    _, near, far = tie((states, near, far))
    tangents = jnp.concatenate([tangents, near, far, *cross(near, far)], axis=0)
    states = states.reshape(-1, tall, columns)
    everyone = (stencil + 1) * count
    send, adv_all, adv_two, route = call(
        functools.partial(forward_kernel, peers, count, stencil),
        [Placed(HBM, (slot_count, *block)), shape((tall, everyone * columns)), shape((tall, wide)),
         Placed(SMEM, (everyone, stencil), jnp.int32)],
        [slots], [states, cubic, w_in, w_out_pad, w_in_t, w_out_t, lam_two], 7 * mix + 11 * net,
        [VMEM(notes, jnp.int32), SMEM(notes, jnp.int32), VMEM((count * stencil, *block), BF), VMEM((hid, wide), F32), sem, sem],
    )
    recv_three = exchange(send)
    _, tangents = tie((send, tangents))
    tangents = jnp.concatenate([tangents, swap(tangents, 1)], axis=0).reshape(-1, tall, columns)
    part_in, part_out, adv_one, hidden_one, slope_one = call(
        between_kernel,
        [shape((channels, hid), F32)] * 2 + [shape((tall, wide))] + [shape((hid, wide))] * 2,
        [], [lam_two, w_in, w_out_t, adv_two, adv_all], 5 * net,
    )
    (pert,) = call(
        functools.partial(tangent_kernel, count, stencil),
        [shape(blocks)], [route], [tangents, cubic, w_in, w_out_pad, adv_all, adv_two], 5 * mix + 15 * net,
    )
    send, mine, give = call(
        functools.partial(third_kernel, *sizes),
        [Placed(HBM, (slot_count, *block)), shape((channels, hid)), shape((channels, hid))],
        [slots, sends],
        [recv_three, cubic, w_in_t, w_out_t, slope_one, hidden_one, adv_one, part_in, part_out], mix + 4 * net,
        [VMEM(blocks, F32), VMEM((count * stencil, *block), BF), sem],
    )
    recv_four = exchange(send)
    mine = add(mine, swap(give, 1))
    step = peers // 2
    if len(steps) % 2:
        mine = add(mine, swap(mine, step))
        step //= 2
    while step > 1:
        near, far, both = swap(mine, step // 2), swap(mine, step), swap(mine, step // 2 * 3)
        mine = ((mine.astype(F32) + near.astype(F32)) + (far.astype(F32) + both.astype(F32))).astype(BF)
        step //= 4
    mine, recv_four, pert = tie((mine, recv_four, pert))
    (back,) = call(functools.partial(last_kernel, slot_count), [shape(blocks, F32)], [sends], [recv_four], net)
    other = swap(mine, 1)
    grad_in = jnp.where(side == 0, mine, other).astype(F32).T
    grad_out = jnp.where(side == 0, other, mine).astype(F32)
    return (pert, back, grad_in, grad_out)


def solution(mesh):
    in_specs = (
        P(("grp", "lat"), None, None),
        P(("grp", "lat"), None, None),
        P(("grp", "lat"), None, None),
        P(),
        P(),
        P(),
        P("grp", "lat", None),
        P("grp", "lat", None, None),
    )
    out_specs = (
        P(("grp", "lat"), None, None),
        P(("grp", "lat"), None, None),
        P("grp", None),
        P("grp", None),
    )
    return jax.shard_map(shards, mesh=mesh, in_specs=in_specs, out_specs=out_specs, check_vma=False)
```

```python
import functools

import jax
import jax.numpy as jnp
from jax import lax
from jax.experimental import pallas as pl
from jax.experimental.pallas import tpu as pltpu
from jax.sharding import PartitionSpec as P

BF = jnp.bfloat16
F32 = jnp.float32
VMEM = pltpu.VMEM
HBM = pltpu.HBM
LANES = 128


def shape(dims, dtype=BF):
    return jax.ShapeDtypeStruct(tuple(dims), dtype)


class Placed:
    def __init__(self, memory_space, dims, dtype=BF):
        self.memory_space, self.shape, self.dtype = memory_space, tuple(dims), jnp.dtype(dtype)
        self.size = functools.reduce(lambda a, b: a * b, self.shape, 1)


SMEM = pltpu.SMEM


def call(kernel, outs, tables, arrays, flops, scratch=()):
    moved = sum(a.size * a.dtype.itemsize for a in arrays) + sum(o.size * o.dtype.itemsize for o in outs)
    places = [o.memory_space if isinstance(o, Placed) else VMEM for o in outs]
    return pl.pallas_call(
        kernel,
        out_shape=tuple(o.memory_space(o.shape, o.dtype) if isinstance(o, Placed) else o for o in outs),
        in_specs=[pl.BlockSpec(memory_space=SMEM)] * len(tables) + [pl.BlockSpec(memory_space=VMEM)] * len(arrays),
        out_specs=tuple(pl.BlockSpec(memory_space=place) for place in places),
        scratch_shapes=list(scratch),
        compiler_params=pltpu.CompilerParams(vmem_limit_bytes=32 * 1024 * 1024),
        cost_estimate=pl.CostEstimate(flops=flops, bytes_accessed=moved, transcendentals=0),
    )(*tables, *arrays)


def dot(a, b):
    return jnp.dot(a, b, preferred_element_type=F32)


def dot_nt(a, b):
    return lax.dot_general(a, b, (((1,), (1,)), ((), ())), preferred_element_type=F32)


def to_rows(wide, count):
    width = wide.shape[1] // count
    return jnp.concatenate([wide[:, j * width : (j + 1) * width] for j in range(count)], axis=0)


def to_lanes(tall, count):
    height = tall.shape[0] // count
    return jnp.concatenate([tall[j * height : (j + 1) * height] for j in range(count)], axis=1)


def gates(preact):
    sigma = 0.5 + 0.5 * jnp.tanh(0.5 * preact)
    hidden = preact * sigma
    return hidden, sigma + hidden * (1.0 - sigma)


def repeat(slots, one):
    if slots <= 16:
        for q in range(slots):
            one(q)
    else:
        pl.loop(0, slots)(one)


def advect(read, count, stencil, cubic_ref):
    parts = [jnp.concatenate([read(t, k) for t in range(count)], axis=0) for k in range(stencil)]
    return to_lanes(dot(jnp.concatenate(parts, axis=1), cubic_ref[...]), count)


def entry_of(sends_ref, section, q):
    cap = sends_ref.shape[2]
    return sends_ref[section, 0, q % cap, q // cap]


def send_terms(ladv, count, stencil, section, slots_ref, cubic_ref, terms_ref, target, sem):
    width = ladv.shape[1] // count
    height = ladv.shape[0]
    terms = dot_nt(to_rows(ladv, count).astype(BF), cubic_ref[...])
    for j in range(count):
        for k in range(stencil):
            block = terms[j * height : (j + 1) * height, k * width : (k + 1) * width]
            terms_ref[j * stencil + k] = block.astype(BF)
            pltpu.make_async_copy(terms_ref.at[j * stencil + k], target(slots_ref[section, j, k]), sem).start()


def collect(sends_ref, section, slots, read, total_ref):
    total_ref[...] = jnp.zeros(total_ref.shape, F32)

    def one(q):
        entry = entry_of(sends_ref, section, q)

        @pl.when(entry >= 0)
        def _():
            total_ref[entry] += read(q).astype(F32)

    repeat(slots, one)


def padded(block, rows):
    block = block.astype(F32)
    if rows == block.shape[0]:
        return block
    return jnp.concatenate([block, jnp.zeros((rows - block.shape[0], block.shape[1]), F32)], axis=0)


def own_kernel(slots_in_ref, sends_in_ref, state_in_ref, out_ref, slots_ref, sends_ref, state_ref, note_ref, sems):
    pairs = ((sends_in_ref, sends_ref), (slots_in_ref, slots_ref), (state_in_ref, state_ref))
    loads = [pltpu.make_async_copy(a, b, sems.at[i]) for i, (a, b) in enumerate(pairs)]
    for load in loads:
        load.start()
    for load in loads:
        load.wait()
    count = state_ref.shape[0]
    rows = out_ref.shape[1]
    notes = [jnp.zeros((1, LANES), F32) for _ in range(-(-(2 * sends_ref.shape[3] + slots_ref[0].size) // LANES))]
    peers, reach = sends_ref.shape[3], slots_ref.shape[2]
    numbers = [(section * peers, sends_ref[section, 0]) for section in range(sends_ref.shape[0])]
    numbers += [(2 * peers + j * reach, slots_ref[0, j : j + 1]) for j in range(count)]
    for start, row in numbers:
        row = row.astype(F32)
        if row.shape[1] < LANES:
            row = jnp.concatenate([row, jnp.zeros((1, LANES - row.shape[1]), F32)], axis=1)
        if start % LANES:
            row = pltpu.roll(row, start % LANES, 1)
        notes[start // LANES] += row
    note_ref[...] = jnp.zeros(note_ref.shape, F32)
    for i, row in enumerate(notes):
        note_ref[i : i + 1] = row
    for j in range(1, count):
        out_ref[j] = padded(state_ref[j], rows).astype(BF)
    top = padded(state_ref[0], rows - 8)
    out_ref[0] = jnp.concatenate([top, note_ref[...]], axis=0).astype(BF)


def own_tangent_kernel(slots_in_ref, sends_in_ref, tangent_in_ref, out_ref, slots_ref, sends_ref, tangent_ref, sems):
    pairs = ((sends_in_ref, sends_ref), (slots_in_ref, slots_ref), (tangent_in_ref, tangent_ref))
    loads = [pltpu.make_async_copy(a, b, sems.at[i]) for i, (a, b) in enumerate(pairs)]
    for load in loads:
        load.start()
    for load in loads:
        load.wait()
    for j in range(tangent_ref.shape[0]):
        out_ref[j] = padded(tangent_ref[j], out_ref.shape[1]).astype(BF)


def prepare_kernel(w_in_t_hbm, w_out_hbm, cubic_hbm, cot_hbm, w_in_ref, w_out_pad_ref, w_out_t_ref, cubic_ref, lam_ref,
                   w_in_t_ref, w_out_ref, cot_ref, sems):
    pairs = ((w_in_t_hbm, w_in_t_ref), (w_out_hbm, w_out_ref), (cot_hbm, cot_ref), (cubic_hbm, cubic_ref))
    loads = [pltpu.make_async_copy(a, b, sems.at[i]) for i, (a, b) in enumerate(pairs)]
    for load in loads:
        load.start()
    for load in loads:
        load.wait()
    lam_ref[...] = side_by_side(cot_ref)
    rows = w_out_pad_ref.shape[0]
    w_in_ref[...] = padded(w_in_t_ref[...], rows).T.astype(BF)
    w_out_pad_ref[...] = padded(w_out_ref[...], rows).astype(BF)
    w_out_t_ref[...] = w_out_ref[...].astype(F32).T.astype(BF)


def routes(peers, count, stencil, slots_ref, blocks_ref, notes_ref, tables_ref, route_ref, sem, meanwhile):
    me = lax.axis_index("lat")
    rows = notes_ref.shape[0] // peers
    under = blocks_ref.shape[1] - 8

    def place(device):
        differs = device ^ me
        return (differs & 1) * (peers // 2) + ((differs >> 1) & 3) * (peers // 8) + (differs >> 3)

    def read_note(r):
        block = blocks_ref[r * count].astype(F32)
        notes_ref[pl.ds(r * rows, rows)] = block[under : under + rows].astype(jnp.int32)

    repeat(peers, read_note)
    copy = pltpu.make_async_copy(notes_ref, tables_ref, sem)
    copy.start()
    meanwhile()
    copy.wait()

    def note(device, start, index):
        return tables_ref[place(device) * rows + start // LANES, start % LANES + index]

    def fill(t, device, block):
        for k in range(stencil):
            owner = note(device, 2 * peers, block * stencil + k)
            entry = jnp.maximum(note(owner, 0, device), 0)
            route_ref[t, k] = place(owner) * count + entry

    for k in range(stencil):
        for j in range(count):
            device = slots_ref[1, j, k]
            fill(k * count + j, device, jnp.maximum(note(device, peers, me), 0))
    for j in range(count):
        fill(stencil * count + j, me, j)


def forward_kernel(peers, count, stencil, slots_ref, blocks_ref, cubic_ref, w_in_ref, w_out_ref, w_in_t_ref, w_out_t_ref, lam_two_ref,
                   send_ref, adv_one_ref, adv_ref, route_ref, notes_ref, tables_ref, terms_ref, pull_ref, sem, note_sem):
    def pull():
        pull_ref[...] = dot(w_out_t_ref[...], lam_two_ref[...])

    routes(peers, count, stencil, slots_ref, blocks_ref, notes_ref, tables_ref, route_ref, note_sem, pull)
    everyone = (stencil + 1) * count
    adv = advect(lambda t, k: blocks_ref[route_ref[t, k]], everyone, stencil, cubic_ref)
    wide = adv.shape[1] // (stencil + 1)
    columns = wide // count
    adv_one_ref[...] = adv.astype(BF)
    fields = []
    for k in range(stencil):
        part = adv_one_ref[:, k * wide : (k + 1) * wide]
        hidden = gates(dot(w_in_ref[...], part))[0].astype(BF)
        fields.append((part.astype(F32) + dot(w_out_ref[...], hidden)).astype(BF))
    adv = advect(lambda j, k: fields[k][:, j * columns : (j + 1) * columns], count, stencil, cubic_ref).astype(BF)
    adv_ref[...] = adv
    lam = lam_two_ref[...]
    slope = gates(dot(w_in_ref[...], adv))[1]
    ghid = (slope * pull_ref[...]).astype(BF)
    ladv = lam.astype(F32) + dot(w_in_t_ref[...], ghid)
    send_terms(ladv, count, stencil, 1, slots_ref, cubic_ref, terms_ref, lambda q: send_ref.at[q], sem)
    pltpu.make_async_copy(terms_ref, terms_ref, sem).wait()


def tangent_kernel(count, stencil, route_ref, blocks_ref, cubic_ref, w_in_ref, w_out_ref, adv_one_ref, adv_two_ref, out_ref):
    def step(adv, tadv):
        slope = gates(dot(w_in_ref[...], adv))[1]
        thid = (slope * dot(w_in_ref[...], tadv)).astype(BF)
        return tadv.astype(F32) + dot(w_out_ref[...], thid)

    tadv = advect(lambda t, k: blocks_ref[route_ref[t, k]], stencil * count, stencil, cubic_ref).astype(BF)
    wide = tadv.shape[1] // stencil
    columns = wide // count
    fields = []
    for k in range(stencil):
        fields.append(step(adv_one_ref[:, k * wide : (k + 1) * wide], tadv[:, k * wide : (k + 1) * wide]).astype(BF))
    tadv = advect(lambda j, k: fields[k][:, j * columns : (j + 1) * columns], count, stencil, cubic_ref).astype(BF)
    pert = step(adv_two_ref[...], tadv)
    channels = out_ref.shape[1]
    for j in range(count):
        out_ref[j] = pert[:channels, j * columns : (j + 1) * columns].astype(BF)


def side_by_side(ref):
    return jnp.concatenate([ref[j] for j in range(ref.shape[0])], axis=1)


def between_kernel(lam_two_ref, w_in_ref, w_out_t_ref, adv_two_ref, adv_all_ref, in_ref, out_ref, adv_one_ref, hidden_ref, slope_ref):
    lam = lam_two_ref[...]
    channels, wide = lam.shape
    adv = adv_two_ref[...]
    hidden, slope = gates(dot(w_in_ref[...], adv))
    ghid = (slope * dot(w_out_t_ref[...], lam)).astype(BF)
    in_ref[...] = dot_nt(adv, ghid)[:channels]
    out_ref[...] = dot_nt(lam, hidden.astype(BF))
    adv = adv_all_ref[:, adv_all_ref.shape[1] - wide :]
    adv_one_ref[...] = adv
    hidden, slope = gates(dot(w_in_ref[...], adv))
    hidden_ref[...] = hidden.astype(BF)
    slope_ref[...] = slope.astype(BF)


def third_kernel(count, stencil, slots, slots_ref, sends_ref, recv_ref, cubic_ref, w_in_t_ref, w_out_t_ref, slope_ref,
                 hidden_ref, adv_ref, part_in_ref, part_out_ref, send_ref, keep_ref, give_ref, total_ref, terms_ref, sem):
    collect(sends_ref, 1, slots, lambda q: recv_ref[q], total_ref)
    lam = side_by_side(total_ref).astype(BF)
    ghid = (slope_ref[...].astype(F32) * dot(w_out_t_ref[...], lam)).astype(BF)
    ladv = lam.astype(F32) + dot(w_in_t_ref[...], ghid)
    send_terms(ladv, count, stencil, 0, slots_ref, cubic_ref, terms_ref, lambda q: send_ref.at[q], sem)
    grad_in = dot_nt(adv_ref[...], ghid)
    grad_in = (part_in_ref[...] + grad_in[: part_in_ref.shape[0]]).astype(BF)
    grad_out = (part_out_ref[...] + dot_nt(lam, hidden_ref[...])).astype(BF)
    side = lax.axis_index("lat") & 1

    @pl.when(side == 0)
    def _():
        keep_ref[...] = grad_in
        give_ref[...] = grad_out

    @pl.when(side != 0)
    def _():
        keep_ref[...] = grad_out
        give_ref[...] = grad_in

    pltpu.make_async_copy(terms_ref, terms_ref, sem).wait()


def last_kernel(slots, sends_ref, recv_ref, back_ref):
    collect(sends_ref, 0, slots, lambda q: recv_ref[q], back_ref)


def shards(state, tangent, cotangent, cubic, w_in, w_out, slots, sends):
    count, channels, columns = state.shape
    stencil = cubic.shape[0]
    hid = w_in.shape[0]
    peers = lax.axis_size("lat")
    slot_count = peers * sends.shape[-1]
    wide = count * columns
    block = (channels, columns)
    blocks = (count, *block)
    side = lax.axis_index("lat") % 2
    sends = jnp.transpose(sends, (0, 1, 3, 2))
    cubic = cubic.reshape(stencil * columns, columns)
    w_in_t = w_in.T
    mix = 2 * wide * channels * stencil * columns
    net = 2 * wide * channels * hid
    sizes = (count, stencil, slot_count)
    sem = pltpu.SemaphoreType.DMA

    def exchange(packed):
        return lax.all_to_all(packed, "lat", split_axis=0, concat_axis=0, tiled=True)

    def swap(values, step):
        return lax.ppermute(values, "lat", [(i, i ^ step) for i in range(peers)])

    def add(a, b):
        return (a.astype(F32) + b.astype(F32)).astype(BF)

    def widen(held, step):
        return jnp.stack([held, swap(held, step)], axis=1).reshape(-1, *held.shape[1:])

    def cross(near, far):
        half = near.shape[0] // 2
        return swap(far[:half], 2), swap(near[half:], 4)

    tie = lax.optimization_barrier

    def load(kernel, arrays, out_shape, scratch):
        return pl.pallas_call(
            kernel,
            out_shape=out_shape,
            in_specs=[pl.BlockSpec(memory_space=HBM)] * len(arrays),
            out_specs=tuple(pl.BlockSpec(memory_space=o.memory_space) for o in out_shape),
            scratch_shapes=scratch,
        )(*(pltpu.with_memory_space_constraint(a, HBM) for a in arrays))

    tall = -(-(channels + 8) // 16) * 16
    note_rows = -(-(2 * peers + count * stencil) // LANES)
    notes = (peers * note_rows, LANES)
    (own,) = load(
        own_kernel, (slots, sends, state), (VMEM((count, tall, columns), BF),),
        [VMEM(slots.shape, slots.dtype), VMEM(sends.shape, sends.dtype), VMEM(blocks, BF), VMEM((8, LANES), F32), sem((3,))],
    )
    steps = []
    while 16 * 2 ** len(steps) <= peers:
        steps.insert(0, 8 * 2 ** len(steps))
    states = own[None]
    for step in steps:
        states = widen(states, step)
    near, far = swap(states, 2), swap(states, 4)
    own, slots, sends = load(
        own_tangent_kernel, (slots, sends, tangent),
        (VMEM((count, tall, columns), BF), SMEM(slots.shape, slots.dtype), SMEM(sends.shape, sends.dtype)),
        [VMEM(blocks, BF), sem((3,))],
    )
    w_in, w_out_pad, w_out_t, cubic, lam_two = load(
        prepare_kernel, (w_in_t, w_out, cubic, cotangent),
        tuple(VMEM(dims, BF) for dims in ((hid, tall), (tall, hid), (hid, channels), cubic.shape, (channels, wide))),
        [VMEM(w_in_t.shape, BF), VMEM(w_out.shape, BF), VMEM(blocks, BF), sem((4,))],
    )
    tangents = own[None]
    for step in steps:
        tangents = widen(tangents, step)
    near, far, tangents = tie((near, far, tangents))
    states = jnp.concatenate([states, near, far, *cross(near, far)], axis=0)
    near, far = swap(tangents, 2), swap(tangents, 4)
    states, w_in, cubic, lam_two = tie((states, w_in, cubic, lam_two))
    states = jnp.concatenate([states, swap(states, 1)], axis=0)
    _, near, far = tie((states, near, far))
    tangents = jnp.concatenate([tangents, near, far, *cross(near, far)], axis=0)
    states = states.reshape(-1, tall, columns)
    everyone = (stencil + 1) * count
    send, adv_all, adv_two, route = call(
        functools.partial(forward_kernel, peers, count, stencil),
        [Placed(HBM, (slot_count, *block)), shape((tall, everyone * columns)), shape((tall, wide)),
         Placed(SMEM, (everyone, stencil), jnp.int32)],
        [slots], [states, cubic, w_in, w_out_pad, w_in_t, w_out_t, lam_two], 7 * mix + 11 * net,
        [VMEM(notes, jnp.int32), SMEM(notes, jnp.int32), VMEM((count * stencil, *block), BF), VMEM((hid, wide), F32), sem, sem],
    )
    recv_three = exchange(send)
    _, tangents = tie((send, tangents))
    tangents = jnp.concatenate([tangents, swap(tangents[: peers // 4], 1), swap(tangents[peers // 4 :], 1)], axis=0)
    tangents = tangents.reshape(-1, tall, columns)
    part_in, part_out, adv_one, hidden_one, slope_one = call(
        between_kernel,
        [shape((channels, hid), F32)] * 2 + [shape((tall, wide))] + [shape((hid, wide))] * 2,
        [], [lam_two, w_in, w_out_t, adv_two, adv_all], 5 * net,
    )
    (pert,) = call(
        functools.partial(tangent_kernel, count, stencil),
        [shape(blocks)], [route], [tangents, cubic, w_in, w_out_pad, adv_all, adv_two], 5 * mix + 15 * net,
    )
    send, mine, give = call(
        functools.partial(third_kernel, *sizes),
        [Placed(HBM, (slot_count, *block)), shape((channels, hid)), shape((channels, hid))],
        [slots, sends],
        [recv_three, cubic, w_in_t, w_out_t, slope_one, hidden_one, adv_one, part_in, part_out], mix + 4 * net,
        [VMEM(blocks, F32), VMEM((count * stencil, *block), BF), sem],
    )
    recv_four = exchange(send)
    mine = add(mine, swap(give, 1))
    step = peers // 2
    if len(steps) % 2:
        mine = add(mine, swap(mine, step))
        step //= 2
    while step > 1:
        near, far, both = swap(mine, step // 2), swap(mine, step), swap(mine, step // 2 * 3)
        mine = ((mine.astype(F32) + near.astype(F32)) + (far.astype(F32) + both.astype(F32))).astype(BF)
        step //= 4
    mine, recv_four, pert = tie((mine, recv_four, pert))
    (back,) = call(functools.partial(last_kernel, slot_count), [shape(blocks, F32)], [sends], [recv_four], net)
    other = swap(mine, 1)
    grad_in = jnp.where(side == 0, mine, other).astype(F32).T
    grad_out = jnp.where(side == 0, other, mine).astype(F32)
    return (pert, back, grad_in, grad_out)


def solution(mesh):
    in_specs = (
        P(("grp", "lat"), None, None),
        P(("grp", "lat"), None, None),
        P(("grp", "lat"), None, None),
        P(),
        P(),
        P(),
        P("grp", "lat", None),
        P("grp", "lat", None, None),
    )
    out_specs = (
        P(("grp", "lat"), None, None),
        P(("grp", "lat"), None, None),
        P("grp", None),
        P("grp", None),
    )
    return jax.shard_map(shards, mesh=mesh, in_specs=in_specs, out_specs=out_specs, check_vma=False)
```
